128 devices in a mesh: cent: 32 (over x, y, core), qry: 4 (over z).
Axes of the slice: x: 4, y: 4, z: 4, core: 2. Of those that a mesh axis runs over, the one named last changes fastest.
Arguments:
- queries: bfloat16 [4, 128, 32, 128], P('qry', 'cent'), may hold values from -0.75 to 0.75
- centroids: bfloat16 [1048576, 128], P('cent'), may hold values from -0.5 to 0.5
- shard_table: int32 [32, 16384], P('cent'), may hold values from 0 to 32767
- token_refs: int32 [4096, 128], P('cent'), may hold values from 0 to 16383
- packed_residual_buckets: int32 [4096, 16, 128], P('cent'), may hold values from 0 to 65280
- passage_lengths: int32 [4096], P('cent'), may hold values from 1 to 128
- bucket_values: float32 [4, 128], replicated, may hold values from -0.75 to 0.75
- candidates: int32 [4, 32, 128, 48], P('qry', 'cent'), may hold values from 0 to 127
- live_counts: int32 [4, 32, 128], P('qry', 'cent'), may hold values from 12 to 36, as said below
Outputs:
- shard_tops: float32 [4, 128, 32, 12], P('qry', 'cent')
- best_scores: float32 [4, 128, 100], P('qry', 'cent')
The draws below stay inside these ranges and needn't reach their ends.
Inputs may be any that keep to these rules, and one draw needn't show every extreme that they name: The bucket of dimension k * 16 + j of token t of passage n is floor(packed_residual_buckets[n, j, t] / 4**k) mod 4, for k = 0..7. Slots 0 to live_counts - 1 of a query's list on a shard are live, the rest padding. On every shard, query i and query 128 - 1 - i of a group hold 48 live slots together, so each device holds 3072 live slots.
All inputs are finite; a program needn't handle non-finite values.
Results may differ from the reference program's by a relative error of at most 0.0003.
Values may be sent and summed in bfloat16 or wider, within the bound.
A program may use at most 128 MiB of HBM per device.

```python
import math
import jax
import jax.numpy as jnp
import numpy as np
from jax import lax

D = 128
QT = 32
PTOK = 128
CENT_DEV = 32768
SLOT = 48
TOPK = 100
PASS_DEV = 128
TABLE_DEV = 16384
DW = 16
KEEP = 12
GROUPS = 4
SHARDS = 32
QG = 128
CENTROIDS = 1048576
PASSAGES = 4096


def draw_live_counts(key, part):
    key = jax.random.fold_in(key, 7)
    first_key, second_key = jax.random.split(key)
    halves = jax.random.randint(first_key, (GROUPS, SHARDS, QG // 2), SLOT // 4, SLOT - SLOT // 4 + 1, dtype=jnp.int32)
    anchor = jax.random.randint(second_key, (GROUPS, SHARDS, 1), 0, QG // 2, dtype=jnp.int32)
    positions = jnp.arange(QG // 2, dtype=jnp.int32)[None, None, :]
    halves = jnp.where(positions == anchor, SLOT // 4, halves)
    return jnp.concatenate([halves, SLOT - halves[:, :, ::-1]], axis=2)


def touch_ends(values, own_key, least, high):
    extent = values.shape
    spot = [jax.random.randint(jax.random.fold_in(own_key, axis), (), 0, extent[axis]) for axis in range(len(extent))]
    values = values.at[tuple(spot)].set(least)
    longest = extent.index(max(extent))
    spot[longest] = (spot[longest] + 1) % extent[longest]
    return values.at[tuple(spot)].set(high)


def levels(key, extent, shards, smallest, top_value):
    level, own = 1.0, jax.random.fold_in(key, 6)
    for axis_at, blocks in shards:
        draws = jnp.exp(jax.random.uniform(jax.random.fold_in(own, axis_at), (blocks,), jnp.float32, smallest / len(shards), top_value / len(shards)))
        level = level * jnp.repeat(draws, extent[axis_at] // blocks).reshape([-1 if axis == axis_at else 1 for axis in range(len(extent))])
    return level


def gaussian(stream_key, shape, deviation, most, cuts=(), held_as=jnp.bfloat16):
    result = jax.random.normal(stream_key, shape, jnp.float32) * deviation
    if len(cuts) > 0:
        result = levels(stream_key, shape, cuts, -0.22, 0.18) * result
    return jnp.clip(result, min=-most, max=most).astype(held_as)


def setup_inputs(seed: int = 0) -> dict:
    arg_keys = jax.random.split(jax.random.key(seed), 10)
    return {
        "queries": gaussian(arg_keys[0], (GROUPS, QG, QT, D), 0.05, 0.75, ((0, 4), (1, 32))),
        "centroids": gaussian(arg_keys[1], (CENTROIDS, D), D ** -0.5, 0.5, ((0, 32),)),
        "shard_table": touch_ends(jax.random.randint(arg_keys[2], (SHARDS, TABLE_DEV), 0, CENT_DEV), jax.random.fold_in(arg_keys[2], 1), 0, CENT_DEV - 1).astype(jnp.int32),
        "token_refs": touch_ends(jax.random.randint(arg_keys[3], (PASSAGES, PTOK), 0, TABLE_DEV), jax.random.fold_in(arg_keys[3], 1), 0, TABLE_DEV - 1).astype(jnp.int32),
        "packed_residual_buckets": touch_ends(jax.random.randint(arg_keys[4], (PASSAGES, DW, PTOK), 0, 65281), jax.random.fold_in(arg_keys[4], 1), 0, 65280).astype(jnp.int32),
        "passage_lengths": touch_ends(jax.random.randint(arg_keys[5], (PASSAGES,), 1, PTOK + 1), jax.random.fold_in(arg_keys[5], 1), 1, PTOK).astype(jnp.int32),
        "bucket_values": gaussian(arg_keys[6], (4, D), 0.05, 0.75, (), jnp.float32),
        "candidates": touch_ends(jax.random.randint(arg_keys[7], (GROUPS, SHARDS, QG, SLOT), 0, PASS_DEV), jax.random.fold_in(arg_keys[7], 1), 0, PASS_DEV - 1).astype(jnp.int32),
        "live_counts": draw_live_counts(jax.random.fold_in(arg_keys[9], 71), 0),
    }


NEG = -1e+30
EPS = 1e-06

def decode_shard(packed_word_bits, token_refs, bucket_values, tablevec):
    powers = jnp.asarray(np.array([4 ** k for k in range(8)], dtype=np.int32))
    digits = packed_word_bits[:, None, :, :] // powers[None, :, None, None] % 4
    digits = digits.reshape(packed_word_bits.shape[0], -1, packed_word_bits.shape[2])
    residual = jnp.zeros(digits.shape, jnp.float32)
    for residual_bucket_number in range(4):
        residual = residual + jnp.where(digits == residual_bucket_number, bucket_values[residual_bucket_number][None, :, None], 0.0)
    cent_tok = jnp.swapaxes(jnp.take(tablevec, token_refs, axis=0), 1, 2).astype(jnp.float32)
    summed = cent_tok + residual
    inverse_norm = lax.rsqrt(lax.optimization_barrier(jnp.sum(summed * summed, axis=1, keepdims=True)) + EPS)
    return (summed * inverse_norm).astype(jnp.bfloat16)

def shard_pairs(embeds, valid_tok, group_queries, slot_cand, slot_count):
    block_size = math.gcd(QG, 16)

    def one_block(first_row):
        query_tile_rows = lax.dynamic_slice_in_dim(group_queries, first_row, block_size, 0).astype(jnp.float32)
        cand_block = lax.dynamic_slice_in_dim(slot_cand, first_row, block_size, 0)
        passage_tile_rows = jnp.take(embeds, cand_block, axis=0).astype(jnp.float32)
        similarity_matrix = jnp.einsum('whu,wpuf->wphf', query_tile_rows, passage_tile_rows)
        token_keep = jnp.take(valid_tok, cand_block, axis=0)[:, :, None, :]
        similarity_matrix = jnp.where(token_keep, similarity_matrix, NEG)
        return lax.optimization_barrier(jnp.sum(lax.optimization_barrier(jnp.max(similarity_matrix, axis=3)), axis=2))
    first_rows = jnp.arange(QG // block_size, dtype=jnp.int32) * block_size
    scores = lax.map(one_block, first_rows).reshape(QG, SLOT)
    live_mask = jnp.arange(SLOT, dtype=jnp.int32)[None, :] < slot_count[:, None]
    return jnp.where(live_mask, scores, NEG)

def reference(queries, centroids, shard_table, token_refs, packed_residual_buckets, passage_lengths, bucket_values, candidates, live_counts):
    per_owner = TABLE_DEV // SHARDS
    owners = jnp.arange(TABLE_DEV, dtype=jnp.int32) // per_owner

    def shard_scores(shard_id):
        offsets = lax.dynamic_index_in_dim(shard_table, shard_id, 0, keepdims=False)
        tablevec = jnp.take(centroids, owners * CENT_DEV + offsets, axis=0)
        first_pass = shard_id * PASS_DEV
        packed_word_bits = lax.dynamic_slice_in_dim(packed_residual_buckets, first_pass, PASS_DEV, 0)
        refs_here = lax.dynamic_slice_in_dim(token_refs, first_pass, PASS_DEV, 0)
        lengths_here = lax.dynamic_slice_in_dim(passage_lengths, first_pass, PASS_DEV, 0)
        embeds = decode_shard(packed_word_bits, refs_here, bucket_values, tablevec)
        valid_tok = jnp.arange(PTOK, dtype=jnp.int32)[None, :] < lengths_here[:, None]
        cand_here = lax.dynamic_index_in_dim(candidates, shard_id, 1, keepdims=False)
        count_here = lax.dynamic_index_in_dim(live_counts, shard_id, 1, keepdims=False)

        def group_scores(inputs):
            return shard_pairs(embeds, valid_tok, inputs[0], inputs[1], inputs[2])
        return lax.map(group_scores, (queries, cand_here, count_here))
    all_scores = lax.map(shard_scores, jnp.arange(SHARDS, dtype=jnp.int32))
    local_tops = lax.top_k(all_scores, KEEP)[0]
    shard_tops = jnp.transpose(local_tops, (1, 2, 0, 3))
    best_scores = lax.top_k(shard_tops.reshape(GROUPS, QG, SHARDS * KEEP), TOPK)[0]
    return (shard_tops, best_scores)
```

```python
import jax
import jax.numpy as jnp
from jax import lax
from jax.experimental import pallas as pl
from jax.experimental.pallas import tpu as pltpu
from jax.sharding import PartitionSpec as P

TOPK = 100
NEG = -1e30
EPS = 1e-6
LOW = float("-inf")
TB = 16
CHUNK = 256
LAG = 3
MESH = pl.DeviceIdType.MESH


def fetch_kernel(
    cent_hbm, wanted, own, tab, qall,
    stage, cent, asked, asked_s, gath, sbuf,
    stage_sem, local_sem, off_send, off_recv, q_send, q_recv, blk_send, blk_recv,
    left_send, right_send, left_recv, right_recv, left_relay, right_relay,
):
    me, z = lax.axis_index("cent"), lax.axis_index("qry")
    n, nz = lax.axis_size("cent"), lax.axis_size("qry")
    right, left = lax.rem(z + 1, nz), lax.rem(z + nz - 1, nz)
    rows = wanted.shape[2]
    pieces = cent_hbm.shape[0] // stage.shape[1]
    depth = stage.shape[1]

    def load(i):
        return pltpu.make_async_copy(
            cent_hbm.at[pl.ds(pl.multiple_of(i * depth, depth), depth)],
            stage.at[lax.rem(i, 2)],
            stage_sem.at[lax.rem(i, 2)],
        )

    load(0).start()
    load(1).start()

    barrier = pltpu.get_barrier_semaphore()

    @pl.loop(1, n)
    def _(i):
        pl.semaphore_signal(barrier, inc=1, device_id=(lax.rem(me + i, n), z), device_id_type=MESH)

    for side in (left, right):
        pl.semaphore_signal(barrier, inc=1, device_id=(me, side), device_id_type=MESH)
    pl.semaphore_wait(barrier, n + 1)

    @pl.loop(1, n)
    def _(i):
        peer = lax.rem(me + i, n)
        pltpu.make_async_remote_copy(
            src_ref=wanted.at[peer], dst_ref=asked.at[me], send_sem=off_send, recv_sem=off_recv,
            device_id=(peer, z), device_id_type=MESH,
        ).start()

    asked[me] = wanted[me]
    qall[me] = own[...]

    @pl.loop(0, pieces)
    def _(i):
        load(i).wait()
        at = pl.multiple_of(i * depth, depth)
        slot = lax.rem(i, 2)

        @pl.loop(0, depth // 256)
        def _(j):
            inner = pl.multiple_of(j * 256, 256)
            cent[pl.ds(at + inner, 256), :] = stage[slot, pl.ds(inner, 256), :].astype(jnp.float32)

        @pl.when(i + 2 < pieces)
        def _():
            load(i + 2).start()

    offsets = pltpu.make_async_remote_copy(
        src_ref=wanted.at[pl.ds(0, n - 1)], dst_ref=asked.at[pl.ds(0, n - 1)],
        send_sem=off_send, recv_sem=off_recv, device_id=(lax.rem(me + 1, n), z), device_id_type=MESH,
    )
    offsets.wait_recv()
    to_scalar = pltpu.make_async_copy(asked, asked_s, local_sem)
    to_scalar.start()
    to_scalar.wait()

    def block_copy(i):
        peer = lax.rem(me + i, n)
        return pltpu.make_async_remote_copy(
            src_ref=sbuf.at[i], dst_ref=tab.at[me, z], send_sem=blk_send, recv_sem=blk_recv.at[i],
            device_id=(peer, z), device_id_type=MESH,
        )

    def along(owner, quarter, side, send, recv):
        return pltpu.make_async_remote_copy(
            src_ref=tab.at[owner, quarter], dst_ref=tab.at[owner, quarter], send_sem=send, recv_sem=recv,
            device_id=(me, side), device_id_type=MESH,
        )

    @pl.loop(0, n + 2 * LAG)
    def _(i):
        @pl.when(i < n)
        def _():
            peer = lax.rem(me + i, n)
            for r in range(rows):
                gath[r : r + 1, :] = cent[pl.ds(asked_s[peer, 0, r], 1), :]

            @pl.when(i == 0)
            def _():
                tab[me, z] = gath[...].astype(jnp.bfloat16)

            @pl.when(i > 0)
            def _():
                sbuf[i] = gath[...].astype(jnp.bfloat16)
                block_copy(i).start()
                pltpu.make_async_remote_copy(
                    src_ref=own, dst_ref=qall.at[me], send_sem=q_send, recv_sem=q_recv,
                    device_id=(peer, z), device_id_type=MESH,
                ).start()

        @pl.when((i >= LAG) & (i < n + LAG))
        def _():
            k = i - LAG
            owner = lax.rem(me + n - k, n)

            @pl.when(k > 0)
            def _():
                block_copy(k).wait_recv()

            along(owner, z, right, right_send, left_recv.at[k]).start()
            along(owner, z, left, left_send, right_recv.at[k]).start()

        @pl.when(i >= 2 * LAG)
        def _():
            k = i - 2 * LAG
            owner = lax.rem(me + n - k, n)
            along(owner, left, right, right_send, left_recv.at[k]).wait_recv()
            along(owner, right, left, left_send, right_recv.at[k]).wait_recv()

            @pl.when(lax.rem(k, 2) == 0)
            def _():
                along(owner, left, right, right_send, left_relay).start()

            @pl.when(lax.rem(k, 2) == 1)
            def _():
                along(owner, right, left, left_send, right_relay).start()

    def bulk(ref, send, recv):
        return pltpu.make_async_remote_copy(
            src_ref=ref, dst_ref=ref, send_sem=send, recv_sem=recv, device_id=(me, right), device_id_type=MESH,
        )

    half = tab.at[pl.ds(0, n // 2 // nz)]
    bulk(half, right_send, left_relay).wait_recv()
    bulk(half, right_send, right_relay).wait_recv()
    bulk(qall.at[pl.ds(0, n - 1)], q_send, q_recv).wait()
    offsets.wait_send()
    bulk(sbuf.at[pl.ds(0, n - 1)], blk_send, q_recv).wait_send()
    sent = tab.at[pl.ds(0, (n + n // 2) // nz)]
    bulk(sent, right_send, left_relay).wait_send()
    bulk(sent, left_send, left_relay).wait_send()


def fetch(centroids, wanted, own):
    n, nz = lax.axis_size("cent"), lax.axis_size("qry")
    rows = wanted.shape[2]
    vmem = pl.BlockSpec(memory_space=pltpu.VMEM)
    dma = pltpu.SemaphoreType.DMA
    return pl.pallas_call(
        fetch_kernel,
        out_shape=(
            jax.ShapeDtypeStruct((n, nz, rows, 128), jnp.bfloat16),
            jax.ShapeDtypeStruct((n,) + own.shape, jnp.bfloat16),
        ),
        in_specs=[pl.BlockSpec(memory_space=pl.ANY), vmem, vmem],
        out_specs=(vmem, vmem),
        scratch_shapes=[
            pltpu.VMEM((2, 4096, 128), jnp.bfloat16),
            pltpu.VMEM(centroids.shape, jnp.float32),
            pltpu.VMEM((n, 1, rows), jnp.int32),
            pltpu.SMEM((n, 1, rows), jnp.int32),
            pltpu.VMEM((rows, 128), jnp.float32),
            pltpu.VMEM((n, rows, 128), jnp.bfloat16),
            dma((2,)), dma, dma, dma, dma, dma, dma, dma((n,)),
            dma, dma, dma((n,)), dma((n,)), dma, dma,
        ],
        compiler_params=pltpu.CompilerParams(
            collective_id=0, has_side_effects=True, vmem_limit_bytes=56 * 2**20
        ),
    )(centroids, wanted, own)


def merge_kernel(tops, shard_out, best_out, outbox, inbox, send_sem, recv_sem):
    me, z = lax.axis_index("cent"), lax.axis_index("qry")
    n = lax.axis_size("cent")
    per = outbox.shape[1]
    keep = shard_out.shape[2]

    barrier = pltpu.get_barrier_semaphore()

    @pl.loop(1, n)
    def _(i):
        pl.semaphore_signal(barrier, inc=1, device_id=(lax.rem(me + i, n), z), device_id_type=MESH)

    for i in range(tops.shape[0] // per):
        outbox[i] = tops[i * per : (i + 1) * per, :]
    inbox[me] = outbox[me]
    pl.semaphore_wait(barrier, n - 1)

    @pl.loop(1, n)
    def _(i):
        peer = lax.rem(me + i, n)
        pltpu.make_async_remote_copy(
            src_ref=outbox.at[peer], dst_ref=inbox.at[me], send_sem=send_sem, recv_sem=recv_sem,
            device_id=(peer, z), device_id_type=MESH,
        ).start()

    pltpu.make_async_remote_copy(
        src_ref=outbox.at[pl.ds(0, n - 1)], dst_ref=inbox.at[pl.ds(0, n - 1)],
        send_sem=send_sem, recv_sem=recv_sem, device_id=(lax.rem(me + 1, n), z), device_id_type=MESH,
    ).wait()

    lists = [inbox[:, q, :] for q in range(per)]
    for q in range(per):
        shard_out[q] = lists[q][:, :keep]
    column = jnp.concatenate(lists, axis=0)
    across = column.T
    width = per * n
    row = across[0:16, :]
    lane = lax.broadcasted_iota(jnp.int32, (16, width), 1)
    shard = lax.rem(lane, n)
    place = lax.broadcasted_iota(jnp.int32, (16, width), 0)

    def count(r, rank):
        near = pltpu.roll(row, r, 1)
        far = pltpu.roll(row, r + width - n, 1)
        other = jnp.where(shard >= r, near, far)
        wrapped = shard < r
        for k in range(keep):
            rival = other[k : k + 1, :]
            ahead = (rival > row) | ((rival == row) & ~wrapped)
            rank = rank + ahead.astype(jnp.int32)
        return rank

    rank = lax.fori_loop(1, n, count, place)
    ranks = jnp.concatenate([rank, jnp.zeros((width - 16, width), jnp.int32)], axis=0).T
    target = lax.broadcasted_iota(jnp.int32, (width, 128), 1)
    found = jnp.zeros((width, 128), jnp.float32)
    for k in range(keep):
        found = found + jnp.where(ranks[:, k : k + 1] == target, column[:, k : k + 1], 0.0)
    for q in range(per):
        best = jnp.sum(found[q * n : (q + 1) * n, :], axis=0, keepdims=True)
        best_out[q : q + 1, :] = best[:, :TOPK]


def merge(tops, per, keep):
    n = lax.axis_size("cent")
    vmem = pl.BlockSpec(memory_space=pltpu.VMEM)
    return pl.pallas_call(
        merge_kernel,
        out_shape=(
            jax.ShapeDtypeStruct((per, n, keep), jnp.float32),
            jax.ShapeDtypeStruct((per, TOPK), jnp.float32),
        ),
        in_specs=[vmem],
        out_specs=(vmem, vmem),
        scratch_shapes=[
            pltpu.VMEM((n, per, 128), jnp.float32),
            pltpu.VMEM((n, per, 128), jnp.float32),
            pltpu.SemaphoreType.DMA,
            pltpu.SemaphoreType.DMA,
        ],
        compiler_params=pltpu.CompilerParams(collective_id=1, has_side_effects=True),
    )(tops)


def score_kernel(
    refs, perm, lens, packed_ref, bv_ref, len_ref, table_ref, q_ref, cand_ref, live_ref,
    out_ref, tab, resid, gath, first, acc, scores, blk_g, blk_b,
):
    passages = packed_ref.shape[0]
    groups = passages // 8
    columns = q_ref.shape[1]
    queries = cand_ref.shape[1]
    slots = cand_ref.shape[0]
    ptok = packed_ref.shape[2]
    rows = TB * 8

    @pl.loop(0, table_ref.shape[0] // 512)
    def _(i):
        at = pl.ds(pl.multiple_of(i * 512, 512), 512)
        tab[at, :] = table_ref[at, :].astype(jnp.float32)

    @pl.loop(0, passages)
    def _(i):
        words = packed_ref[perm[i]]
        digits = jnp.concatenate([(words >> (2 * k)) & 3 for k in range(8)], axis=0)
        low = jnp.where(digits == 0, bv_ref[0], bv_ref[1])
        high = jnp.where(digits == 2, bv_ref[2], bv_ref[3])
        value = jnp.where(digits < 2, low, high)
        base = lax.div(i, 8) * (8 * ptok) + lax.rem(i, 8)
        resid[pl.ds(base, ptok, stride=8), :] = value.T

    acc[...] = jnp.full(acc.shape, LOW, jnp.float32)

    def add_group(g, n):
        count = lax.div(lens[g * 8] + (TB - 1), TB)

        def add(b, m):
            blk_g[m] = g
            blk_b[m] = b
            return m + 1

        return lax.fori_loop(0, count, add, n)

    total = lax.fori_loop(0, groups, add_group, 0)

    def embed(i):
        g, b = blk_g[i], blk_b[i]
        where = [perm[g * 8 + p] * ptok + b * TB for p in range(8)]
        for t in range(TB):
            for p in range(8):
                gath[pl.ds(t * 8 + p, 1), :] = tab[pl.ds(refs[where[p] + t], 1), :]
        start = pl.multiple_of(g * (8 * ptok) + b * rows, rows)
        summed = gath[...] + resid[pl.ds(start, rows), :]
        norm = jnp.sum(summed * summed, axis=1, keepdims=True)
        unit = (summed * lax.rsqrt(norm + EPS)).reshape(TB, 8, 128)
        head = jnp.where(b == 0, unit[0], first[...])
        first[...] = head
        token = b * TB + lax.broadcasted_iota(jnp.int32, (TB, 8, 128), 0)
        unit = jnp.where(token < len_ref[g][None], unit, head[None])
        return unit.reshape(rows, 128).astype(jnp.bfloat16)

    def step(i, unit):
        g = blk_g[i]
        following = embed(jnp.minimum(i + 1, total - 1))
        for c in range(0, columns, CHUNK):
            sim = jnp.dot(unit, q_ref[:, c : c + CHUNK], preferred_element_type=jnp.float32)
            best = jnp.max(sim.reshape(TB, 8, CHUNK), axis=0)
            acc[g, :, c : c + CHUNK] = jnp.maximum(acc[g, :, c : c + CHUNK], best)
        return following

    lax.fori_loop(0, total, step, embed(0))

    @pl.loop(0, groups)
    def _(g):
        total_sum = acc[g, :, 0:queries]
        for t in range(1, columns // queries):
            total_sum = total_sum + acc[g, :, t * queries : (t + 1) * queries]
        scores[pl.ds(pl.multiple_of(g * 8, 8), 8), :] = total_sum

    cand = cand_ref[...]

    def pick(r, picked):
        return jnp.where(cand == perm[r], scores[pl.ds(r, 1), :], picked)

    picked = lax.fori_loop(0, passages, pick, jnp.zeros((slots, queries), jnp.float32), unroll=8)
    place = lax.broadcasted_iota(jnp.int32, (slots, queries), 0)
    values = jnp.where(place < live_ref[...], picked, NEG)
    place_out = lax.broadcasted_iota(jnp.int32, (16, queries), 0)
    tops = jnp.zeros((16, queries), jnp.float32)
    for k in range(slots // 4):
        top = jnp.max(values, axis=0, keepdims=True)
        tops = jnp.where(place_out == k, top, tops)
        at = jnp.min(jnp.where(values == top, place, slots), axis=0, keepdims=True)
        values = jnp.where(place == at, LOW, values)
    padded = jnp.concatenate([tops, jnp.zeros((128 - 16, queries), jnp.float32)], axis=0)
    out_ref[...] = padded.T


def local_scores(table, refs, packed, lengths, bucket_values, qcols, cand, live):
    passages, _, ptok = packed.shape
    queries, slots = cand.shape
    perm = jnp.argsort(-lengths).astype(jnp.int32)
    lens = lengths[perm]
    len_rows = jnp.broadcast_to(lens.reshape(passages // 8, 8, 1), (passages // 8, 8, 128))
    bv = jnp.broadcast_to(bucket_values[:, :, None], (4, 128, ptok))
    vmem = pl.BlockSpec(memory_space=pltpu.VMEM)
    smem = pl.BlockSpec(memory_space=pltpu.SMEM)
    blocks = passages // 8 * (ptok // TB)
    return pl.pallas_call(
        score_kernel,
        out_shape=jax.ShapeDtypeStruct((queries, 128), jnp.float32),
        in_specs=[smem, smem, smem, vmem, vmem, vmem, vmem, vmem, vmem, vmem],
        out_specs=vmem,
        scratch_shapes=[
            pltpu.VMEM((table.shape[0], 128), jnp.float32),
            pltpu.VMEM((passages * ptok, 128), jnp.float32),
            pltpu.VMEM((TB * 8, 128), jnp.float32),
            pltpu.VMEM((8, 128), jnp.float32),
            pltpu.VMEM((passages // 8, 8, qcols.shape[1]), jnp.float32),
            pltpu.VMEM((passages, queries), jnp.float32),
            pltpu.SMEM((blocks,), jnp.int32),
            pltpu.SMEM((blocks,), jnp.int32),
        ],
        compiler_params=pltpu.CompilerParams(vmem_limit_bytes=56 * 2**20),
    )(refs.reshape(-1), perm, lens, packed, bv, len_rows, table, qcols, cand.T, live[None, :])


def local(
    queries,
    centroids,
    shard_table,
    token_refs,
    packed_residual_buckets,
    passage_lengths,
    bucket_values,
    candidates,
    live_counts,
):
    n, nz = lax.axis_size("cent"), lax.axis_size("qry")
    per, tokens, width = queries.shape[1:]
    by_owner = shard_table.reshape(n, nz, -1)
    wanted = lax.dynamic_slice_in_dim(by_owner, lax.axis_index("qry"), 1, 1)
    table, everyone = fetch(centroids, wanted, queries.reshape(per * tokens, width))
    qcols = jnp.transpose(everyone.reshape(n * per, tokens, width), (2, 1, 0)).reshape(width, -1)
    tops = local_scores(
        table.reshape(-1, width), token_refs, packed_residual_buckets, passage_lengths, bucket_values, qcols,
        candidates[0, 0], live_counts[0, 0],
    )
    shard_tops, best_scores = merge(tops, per, candidates.shape[3] // 4)
    return (shard_tops[None], best_scores[None])


def solution(mesh):
    return jax.shard_map(
        local,
        mesh=mesh,
        in_specs=(
            P("qry", "cent", None, None),
            P("cent", None),
            P("cent", None),
            P("cent", None),
            P("cent", None, None),
            P("cent"),
            P(),
            P("qry", "cent", None, None),
            P("qry", "cent", None),
        ),
        out_specs=(P("qry", "cent", None, None), P("qry", "cent", None)),
        check_vma=False,
    )
```

```python
import jax
import jax.numpy as jnp
from jax import lax
from jax.experimental import pallas as pl
from jax.experimental.pallas import tpu as pltpu
from jax.sharding import PartitionSpec as P

TOPK = 100
NEG = -1e30
EPS = 1e-6
LOW = float("-inf")
TB = 16
CHUNK = 512
UNIT = 4
MESH = pl.DeviceIdType.MESH


def fetch_kernel(
    cent_hbm, wanted, own, lengths, packed, buckets, tab, resid_hbm, qcols, order,
    stage, cent, asked, asked_s, sbuf, qall, qwide, spread, resid, order_s,
    stage_sem, asked_sem, order_sem, own_sem, resid_sem, off_send, off_recv,
    q_send, q_recv, pair_send, pair_recv, blk_send, blk_recv, half_recv, z_send, left_recv, right_recv, far_recv,
):
    me, z = lax.axis_index("cent"), lax.axis_index("qry")
    n, nz = lax.axis_size("cent"), lax.axis_size("qry")
    core = lax.rem(me, 2)
    chip = lax.div(me, 2)
    chips = n // 2
    right, far, left = lax.rem(z + 1, nz), lax.rem(z + 2, nz), lax.rem(z + 3, nz)
    rows = tab.shape[2]
    part = sbuf.shape[1] - rows
    pieces = stage_sem.shape[0]
    depth = stage.shape[0] // pieces
    passages = packed.shape[0]
    ptok = packed.shape[2]

    loads = [
        pltpu.make_async_copy(
            cent_hbm.at[i * depth : (i + 1) * depth], stage.at[i * depth : (i + 1) * depth], stage_sem.at[i]
        )
        for i in range(pieces)
    ]
    for load in loads:
        load.start()

    barrier = pltpu.get_barrier_semaphore()

    @pl.loop(1, n)
    def _(i):
        pl.semaphore_signal(barrier, inc=1, device_id=(lax.rem(me + i, n), z), device_id_type=MESH)

    for side in (left, right, far):
        pl.semaphore_signal(barrier, inc=1, device_id=(me, side), device_id_type=MESH)

    across = jnp.broadcast_to(lengths[...], (passages, passages))
    down = across.T
    line = lax.broadcasted_iota(jnp.int32, (passages, passages), 0)
    lane = lax.broadcasted_iota(jnp.int32, (passages, passages), 1)
    ahead = (down > across) | ((down == across) & (line < lane))
    rank = jnp.sum(ahead.astype(jnp.int32), axis=0, keepdims=True)
    hit = jnp.broadcast_to(rank, (passages, passages)).T == lane
    order[0:1, :] = jnp.sum(jnp.where(hit, line, 0), axis=0, keepdims=True)
    order[1:2, :] = jnp.sum(jnp.where(hit, down, 0), axis=0, keepdims=True)
    order[2:8, :] = jnp.zeros((6, passages), jnp.int32)
    to_order = pltpu.make_async_copy(order, order_s, order_sem)
    to_order.start()
    for b in range(4):
        spread[b] = jnp.broadcast_to(buckets[b : b + 1, :], (ptok, 128)).T

    def widen(first, last):
        for i in range(first, last):
            loads[i].wait()

            @pl.loop(0, depth // 512)
            def _(j):
                at = pl.ds(pl.multiple_of(i * depth + j * 512, 512), 512)
                cent[at, :] = stage[at, :].astype(jnp.float32)

    widen(0, pieces // 2)
    pl.semaphore_wait(barrier, n + 2)

    @pl.loop(1, n)
    def _(i):
        peer = lax.rem(me + i, n)
        pltpu.make_async_remote_copy(
            src_ref=wanted.at[peer], dst_ref=asked.at[me], send_sem=off_send, recv_sem=off_recv,
            device_id=(peer, z), device_id_type=MESH,
        ).start()

    asked[me] = wanted[me]
    qall[chip, core] = own[...]
    widen(pieces // 2, pieces)
    to_order.wait()

    offsets = pltpu.make_async_remote_copy(
        src_ref=wanted.at[pl.ds(0, n - 1)], dst_ref=asked.at[pl.ds(0, n - 1)],
        send_sem=off_send, recv_sem=off_recv, device_id=(lax.rem(me + 1, n), z), device_id_type=MESH,
    )
    offsets.wait_recv()
    to_scalar = pltpu.make_async_copy(asked, asked_s, asked_sem)
    to_scalar.start()
    to_scalar.wait()

    sub = lax.broadcasted_iota(jnp.int32, (16, 128), 0)

    def pull(i, line, start, count):
        peer = lax.rem(me + i, n)
        for r in range(0, count, 16):
            tile = jnp.broadcast_to(cent[pl.ds(asked_s[peer, line, r], 1), :], (16, 128))
            for k in range(1, 16):
                value = jnp.broadcast_to(cent[pl.ds(asked_s[peer, line, r + k], 1), :], (16, 128))
                tile = jnp.where(sub == k, value, tile)
            sbuf[i, start + r : start + r + 16, :] = tile.astype(jnp.bfloat16)

    def block_copy(i):
        return pltpu.make_async_remote_copy(
            src_ref=sbuf.at[i, pl.ds(0, rows)], dst_ref=tab.at[me, z], send_sem=blk_send, recv_sem=blk_recv.at[i],
            device_id=(lax.rem(me + i, n), z), device_id_type=MESH,
        )

    pull(0, 0, 0, rows)
    keep_own = pltpu.make_async_copy(sbuf.at[0, pl.ds(0, rows)], tab.at[me, z], own_sem.at[0])
    keep_own.start()

    @pl.loop(1, n)
    def _(i):
        pull(i, 0, 0, rows)
        block_copy(i).start()

    def along(ref, side, recv):
        return pltpu.make_async_remote_copy(
            src_ref=ref, dst_ref=ref, send_sem=z_send, recv_sem=recv, device_id=(me, side), device_id_type=MESH,
        )

    def forward(k):
        owner = lax.rem(me + n - k, n)
        along(tab.at[owner, z], right, left_recv).start()
        along(tab.at[owner, z], left, right_recv).start()
        along(tab.at[owner, z, pl.ds(part, rows - part)], far, far_recv).start()

    def decode(i):
        words = packed[order_s[0, i]]
        digits = jnp.concatenate([(words >> (2 * k)) & 3 for k in range(8)], axis=0)
        low = jnp.where(digits == 0, spread[0], spread[1])
        high = jnp.where(digits == 2, spread[2], spread[3])
        value = jnp.where(digits < 2, low, high)
        resid[lax.div(i, 8), pl.ds(lax.rem(i, 8), ptok, stride=8), :] = value.T

    def extras(k):
        for j in range(passages // n):
            decode(k * (passages // n) + j)
        pull(k, 1, rows, part)

    def save(g):
        return pltpu.make_async_copy(resid.at[g], resid_hbm.at[g], resid_sem)

    keep_own.wait()
    forward(0)
    extras(0)
    keep_half = pltpu.make_async_copy(sbuf.at[0, pl.ds(rows, part)], tab.at[me, far, pl.ds(0, part)], own_sem.at[1])
    keep_half.start()

    @pl.loop(1, n)
    def _(k):
        block_copy(k).wait_recv()
        forward(k)
        extras(k)
        pltpu.make_async_remote_copy(
            src_ref=sbuf.at[k, pl.ds(rows, part)], dst_ref=tab.at[me, far, pl.ds(0, part)],
            send_sem=blk_send, recv_sem=half_recv,
            device_id=(lax.rem(me + k, n), z), device_id_type=MESH,
        ).start()

        @pl.when(lax.rem(k, 2) == 0)
        def _():
            pltpu.make_async_remote_copy(
                src_ref=own, dst_ref=qall.at[chip, core], send_sem=q_send, recv_sem=q_recv,
                device_id=(lax.rem(me + k, n), z), device_id_type=MESH,
            ).start()

        @pl.when(lax.rem(k, 2) == 1)
        def _():
            save(lax.div(k, 2)).start()

    def bulk(ref, send, recv):
        return pltpu.make_async_remote_copy(
            src_ref=ref, dst_ref=ref, send_sem=send, recv_sem=recv, device_id=(me, right), device_id_type=MESH,
        )

    bulk(qall.at[pl.ds(0, chips - 1), 0], q_send, q_recv).wait_recv()
    pair = pltpu.make_async_remote_copy(
        src_ref=qall.at[pl.ds(0, chips), core], dst_ref=qall.at[pl.ds(0, chips), core],
        send_sem=pair_send, recv_sem=pair_recv,
        device_id=(me + 1 - 2 * core, z), device_id_type=MESH,
    )
    pair.start()
    pair.wait()

    tokens = own.shape[0] * n // passages
    per = own.shape[0]

    @pl.loop(0, chips)
    def _(i):
        for c in range(2):
            qwide[pl.ds(pl.multiple_of((i * 2 + c) * per, per), per), :] = qall[i, c].astype(jnp.float32)

    for t in range(tokens):
        tile = qwide[pl.ds(t, passages, stride=tokens), :]
        qcols[:, t * passages : (t + 1) * passages] = tile.T.astype(jnp.bfloat16)

    bulk(tab.at[pl.ds(0, n // nz)], z_send, left_recv).wait_recv()
    bulk(tab.at[pl.ds(0, n // nz)], z_send, right_recv).wait_recv()
    bulk(tab.at[pl.ds(0, n), 0, pl.ds(part, rows - part)], z_send, far_recv).wait_recv()
    bulk(sbuf.at[pl.ds(0, n - 1), pl.ds(rows, part)], z_send, half_recv).wait_recv()
    keep_half.wait()
    pltpu.make_async_copy(resid, resid_hbm, resid_sem).wait()
    offsets.wait_send()
    bulk(qall.at[pl.ds(0, chips - 1), 0], q_send, q_recv).wait_send()
    bulk(sbuf.at[pl.ds(0, n - 1)], blk_send, q_recv).wait_send()
    bulk(tab.at[pl.ds(0, 2 * n // nz)], z_send, q_recv).wait_send()
    bulk(tab.at[pl.ds(0, n), 0, pl.ds(part, rows - part)], z_send, q_recv).wait_send()


def fetch(centroids, wanted, own, lengths, packed, buckets):
    n, nz = lax.axis_size("cent"), lax.axis_size("qry")
    rows = wanted.shape[2]
    part = rows // 2
    passages, _, ptok = packed.shape
    vmem = pl.BlockSpec(memory_space=pltpu.VMEM)
    hbm = pl.BlockSpec(memory_space=pl.ANY)
    dma = pltpu.SemaphoreType.DMA
    groups = passages // 8
    return pl.pallas_call(
        fetch_kernel,
        out_shape=(
            jax.ShapeDtypeStruct((n, nz, rows, 128), jnp.bfloat16),
            jax.ShapeDtypeStruct((groups, 8 * ptok, 128), jnp.float32),
            jax.ShapeDtypeStruct((128, n * own.shape[0]), jnp.bfloat16),
            jax.ShapeDtypeStruct((8, passages), jnp.int32),
        ),
        in_specs=[hbm, vmem, vmem, vmem, vmem, vmem],
        out_specs=(hbm, hbm, vmem, vmem),
        scratch_shapes=[
            pltpu.VMEM(centroids.shape, jnp.bfloat16),
            pltpu.VMEM(centroids.shape, jnp.float32),
            pltpu.VMEM((n, 2, rows), jnp.int32),
            pltpu.SMEM((n, 2, rows), jnp.int32),
            pltpu.VMEM((n, rows + part, 128), jnp.bfloat16),
            pltpu.VMEM((n // 2, 2) + own.shape, jnp.bfloat16),
            pltpu.VMEM((n * own.shape[0], 128), jnp.float32),
            pltpu.VMEM((4, 128, ptok), jnp.float32),
            pltpu.VMEM((groups, 8 * ptok, 128), jnp.float32),
            pltpu.SMEM((8, passages), jnp.int32),
            dma((8,)), dma, dma, dma((2,)), dma, dma, dma,
            dma, dma, dma, dma, dma, dma((n,)), dma, dma, dma, dma, dma,
        ],
        compiler_params=pltpu.CompilerParams(
            collective_id=0, has_side_effects=True, vmem_limit_bytes=58 * 2**20
        ),
    )(centroids, wanted, own, lengths, packed, buckets)


def score_kernel(
    refs, order, order_ref, table_hbm, resid_hbm, q_hbm, cand_ref, live_ref,
    out_ref, stage, tab, resid, q_ref, first, acc, scores, len_ref, blk_g, blk_b, stage_sem, resid_sem, q_sem,
):
    passages = order.shape[1]
    groups = passages // 8
    columns = q_ref.shape[1]
    slots, queries = cand_ref.shape
    ptok = resid_hbm.shape[1] // 8
    rows = TB * 8
    pieces = stage_sem.shape[0]
    depth = stage.shape[0] // pieces

    def load(i):
        return pltpu.make_async_copy(
            table_hbm.at[pl.ds(pl.multiple_of(i * depth, depth), depth)],
            stage.at[lax.rem(i, 2)], stage_sem.at[lax.rem(i, 2)],
        )

    loads = [
        pltpu.make_async_copy(
            table_hbm.at[i * depth : (i + 1) * depth], stage.at[i * depth : (i + 1) * depth], stage_sem.at[i]
        )
        for i in range(pieces)
    ]
    for load in loads:
        load.start()
    load_q = pltpu.make_async_copy(q_hbm, q_ref, q_sem)
    load_q.start()

    def load_resid(g):
        return pltpu.make_async_copy(resid_hbm.at[g], resid.at[g], resid_sem.at[g])

    @pl.loop(0, groups)
    def _(g):
        load_resid(g).start()

    acc[...] = jnp.full(acc.shape, LOW, jnp.float32)
    spread = jnp.broadcast_to(order_ref[1:2, :], (passages, passages)).T
    len_ref[...] = spread.reshape(groups, 8, 128)

    def add_group(g, n):
        count = lax.div(order[1, g * 8] + (TB - 1), TB)

        def add(b, m):
            blk_g[m] = g
            blk_b[m] = b
            return m + 1

        return lax.fori_loop(0, count, add, n)

    total = lax.fori_loop(0, groups, add_group, 0)
    for extra in range(UNIT - 1):
        blk_g[total + extra] = blk_g[total - 1]
        blk_b[total + extra] = blk_b[total - 1]
    steps = lax.div(total + (UNIT - 1), UNIT)

    for i, load in enumerate(loads):
        load.wait()

        @pl.loop(0, depth // 512)
        def _(j):
            at = pl.ds(pl.multiple_of(i * depth + j * 512, 512), 512)
            tab[at, :] = stage[at, :].astype(jnp.float32)

    load_q.wait()

    def arrive(first_group, last_group):
        @pl.loop(first_group, last_group + 1)
        def _(g):
            load_resid(g).wait()

    arrive(0, blk_g[UNIT - 1])

    def embed_one(u, i, head):
        g, b = blk_g[i], blk_b[i]
        where = [order[0, g * 8 + p] * ptok + b * TB for p in range(8)]
        sub = lax.broadcasted_iota(jnp.int32, (8, 128), 0)
        tiles = []
        for t in range(TB):
            tile = jnp.broadcast_to(tab[pl.ds(refs[where[0] + t], 1), :], (8, 128))
            for p in range(1, 8):
                tile = jnp.where(sub == p, jnp.broadcast_to(tab[pl.ds(refs[where[p] + t], 1), :], (8, 128)), tile)
            tiles.append(tile)
        got = jnp.concatenate(tiles, axis=0)
        start = pl.multiple_of(b * rows, rows)
        summed = got + resid[g, pl.ds(start, rows), :]
        norm = jnp.sum(summed * summed, axis=1, keepdims=True)
        unit = (summed * lax.rsqrt(norm + EPS)).reshape(TB, 8, 128)
        head = jnp.where(b == 0, unit[0], head)
        token = b * TB + lax.broadcasted_iota(jnp.int32, (TB, 8, 128), 0)
        unit = jnp.where(token < len_ref[g][None], unit, head[None])
        return unit.reshape(rows, 128).astype(jnp.bfloat16), head

    def embed(s):
        head = first[...]
        units = []
        for u in range(UNIT):
            unit, head = embed_one(u, s * UNIT + u, head)
            units.append(unit)
        first[...] = head
        return jnp.concatenate(units, axis=0)

    def step(s, unit):
        later = jnp.minimum(s + 1, steps - 1)
        arrive(blk_g[s * UNIT + UNIT - 1] + 1, blk_g[later * UNIT + UNIT - 1])
        group = [blk_g[s * UNIT + u] for u in range(UNIT)]
        head = first[...]
        following = []
        parts = columns // CHUNK // UNIT
        for part, c in enumerate(range(0, columns, CHUNK)):
            if part % parts == 0:
                u = part // parts
                block, head = embed_one(u, later * UNIT + u, head)
                following.append(block)
            sim = jnp.dot(unit, q_ref[:, c : c + CHUNK], preferred_element_type=jnp.float32)
            best = jnp.max(sim.reshape(UNIT, TB, 8, CHUNK), axis=1)
            for u in range(UNIT):
                acc[group[u], :, c : c + CHUNK] = jnp.maximum(acc[group[u], :, c : c + CHUNK], best[u])
        first[...] = head
        return jnp.concatenate(following, axis=0)

    lax.fori_loop(0, steps, step, embed(0))

    @pl.loop(0, groups)
    def _(g):
        total_sum = acc[g, :, 0:queries]
        for t in range(1, columns // queries):
            total_sum = total_sum + acc[g, :, t * queries : (t + 1) * queries]
        scores[pl.ds(pl.multiple_of(g * 8, 8), 8), :] = total_sum

    cand = cand_ref[...]

    def pick(r, picked):
        return jnp.where(cand == order[0, r], scores[pl.ds(r, 1), :], picked)

    picked = lax.fori_loop(0, passages, pick, jnp.zeros((slots, queries), jnp.float32), unroll=8)
    place = lax.broadcasted_iota(jnp.int32, (slots, queries), 0)
    values = jnp.where(place < live_ref[...], picked, NEG)
    place_out = lax.broadcasted_iota(jnp.int32, (16, queries), 0)
    tops = jnp.zeros((16, queries), jnp.float32)
    for k in range(slots // 4):
        top = jnp.max(values, axis=0, keepdims=True)
        tops = jnp.where(place_out == k, top, tops)
        at = jnp.min(jnp.where(values == top, place, slots), axis=0, keepdims=True)
        values = jnp.where(place == at, LOW, values)
    padded = jnp.concatenate([tops, jnp.zeros((128 - 16, queries), jnp.float32)], axis=0)
    out_ref[...] = padded.T


def score(table, refs, order, resid, qcols, cand, live):
    groups = resid.shape[0]
    passages = order.shape[1]
    queries, slots = cand.shape
    vmem = pl.BlockSpec(memory_space=pltpu.VMEM)
    smem = pl.BlockSpec(memory_space=pltpu.SMEM)
    hbm = pl.BlockSpec(memory_space=pl.ANY)
    blocks = resid.shape[0] * resid.shape[1] // (8 * TB) + UNIT
    return pl.pallas_call(
        score_kernel,
        out_shape=jax.ShapeDtypeStruct((queries, 128), jnp.float32),
        in_specs=[smem, smem, vmem, hbm, hbm, hbm, vmem, vmem],
        out_specs=vmem,
        scratch_shapes=[
            pltpu.VMEM(table.shape, jnp.bfloat16),
            pltpu.VMEM((table.shape[0], 128), jnp.float32),
            pltpu.VMEM(resid.shape, jnp.float32),
            pltpu.VMEM(qcols.shape, jnp.bfloat16),
            pltpu.VMEM((8, 128), jnp.float32),
            pltpu.VMEM((groups, 8, qcols.shape[1]), jnp.float32),
            pltpu.VMEM((passages, queries), jnp.float32),
            pltpu.VMEM((groups, 8, 128), jnp.int32),
            pltpu.SMEM((blocks,), jnp.int32),
            pltpu.SMEM((blocks,), jnp.int32),
            pltpu.SemaphoreType.DMA((8,)),
            pltpu.SemaphoreType.DMA((groups,)),
            pltpu.SemaphoreType.DMA,
        ],
        compiler_params=pltpu.CompilerParams(vmem_limit_bytes=56 * 2**20),
    )(refs.reshape(-1), order, order, table, resid, qcols, cand.T, live[None, :])


def swap_kernel(tops, inbox, outbox, send_sem, recv_sem):
    me, z = lax.axis_index("cent"), lax.axis_index("qry")
    n = lax.axis_size("cent")
    per = outbox.shape[1]
    barrier = pltpu.get_barrier_semaphore()

    @pl.loop(1, n)
    def _(i):
        pl.semaphore_signal(barrier, inc=1, device_id=(lax.rem(me + i, n), z), device_id_type=MESH)

    for i in range(tops.shape[0] // per):
        outbox[i] = tops[i * per : (i + 1) * per, :]
    inbox[me] = outbox[me]
    pl.semaphore_wait(barrier, n - 1)

    @pl.loop(1, n)
    def _(i):
        peer = lax.rem(me + i, n)
        pltpu.make_async_remote_copy(
            src_ref=outbox.at[peer], dst_ref=inbox.at[me], send_sem=send_sem, recv_sem=recv_sem,
            device_id=(peer, z), device_id_type=MESH,
        ).start()

    pltpu.make_async_remote_copy(
        src_ref=outbox.at[pl.ds(0, n - 1)], dst_ref=inbox.at[pl.ds(0, n - 1)],
        send_sem=send_sem, recv_sem=recv_sem, device_id=(lax.rem(me + 1, n), z), device_id_type=MESH,
    ).wait()


def swap(tops, per):
    n = lax.axis_size("cent")
    vmem = pl.BlockSpec(memory_space=pltpu.VMEM)
    return pl.pallas_call(
        swap_kernel,
        out_shape=jax.ShapeDtypeStruct((n, per, 128), jnp.float32),
        in_specs=[vmem],
        out_specs=vmem,
        scratch_shapes=[
            pltpu.VMEM((n, per, 128), jnp.float32),
            pltpu.SemaphoreType.DMA,
            pltpu.SemaphoreType.DMA,
        ],
        compiler_params=pltpu.CompilerParams(collective_id=1, has_side_effects=True),
    )(tops)


def merge_kernel(inbox, shard_out, best_out):
    n, per = inbox.shape[:2]
    keep = shard_out.shape[2]
    lists = [inbox[:, q, :] for q in range(per)]
    for q in range(per):
        shard_out[q] = lists[q][:, :keep]
    column = jnp.concatenate(lists, axis=0)
    across = column.T
    width = per * n
    row = across[0:16, :]
    lane = lax.broadcasted_iota(jnp.int32, (16, width), 1)
    shard = lax.rem(lane, n)
    place = lax.broadcasted_iota(jnp.int32, (16, width), 0)

    def count(r, rank):
        near = pltpu.roll(row, r, 1)
        far = pltpu.roll(row, r + width - n, 1)
        wrapped = shard < r
        other = jnp.where(wrapped, far, near)
        for k in range(keep):
            rival = other[k : k + 1, :]
            ahead = (rival > row) | ((rival == row) & ~wrapped)
            rank = rank + ahead.astype(jnp.int32)
        return rank

    rank = lax.fori_loop(1, n, count, place)
    ranks = jnp.concatenate([rank, jnp.zeros((width - 16, width), jnp.int32)], axis=0).T
    target = lax.broadcasted_iota(jnp.int32, (width, 128), 1)
    found = jnp.zeros((width, 128), jnp.float32)
    for k in range(keep):
        found = found + jnp.where(ranks[:, k : k + 1] == target, column[:, k : k + 1], 0.0)
    for q in range(per):
        best = jnp.sum(found[q * n : (q + 1) * n, :], axis=0, keepdims=True)
        best_out[q : q + 1, :] = best[:, :TOPK]


def merge(inbox, keep):
    n, per, _ = inbox.shape
    vmem = pl.BlockSpec(memory_space=pltpu.VMEM)
    return pl.pallas_call(
        merge_kernel,
        out_shape=(
            jax.ShapeDtypeStruct((per, n, keep), jnp.float32),
            jax.ShapeDtypeStruct((per, TOPK), jnp.float32),
        ),
        in_specs=[vmem],
        out_specs=(vmem, vmem),
    )(inbox)


def local(
    queries,
    centroids,
    shard_table,
    token_refs,
    packed_residual_buckets,
    passage_lengths,
    bucket_values,
    candidates,
    live_counts,
):
    n, nz = lax.axis_size("cent"), lax.axis_size("qry")
    per, tokens, width = queries.shape[1:]
    z = lax.axis_index("qry")
    by_owner = shard_table.reshape(n, nz, -1)
    wanted = jnp.concatenate(
        [lax.dynamic_slice_in_dim(by_owner, quarter, 1, 1) for quarter in (z, lax.rem(z + 2, nz))], axis=1
    )
    table, resid, qcols, order = fetch(
        centroids, wanted, queries.reshape(per * tokens, width), passage_lengths[None, :], packed_residual_buckets,
        bucket_values,
    )
    tops = score(table.reshape(-1, width), token_refs, order, resid, qcols, candidates[0, 0], live_counts[0, 0])
    shard_tops, best_scores = merge(swap(tops, per), candidates.shape[3] // 4)
    return (shard_tops[None], best_scores[None])


def solution(mesh):
    return jax.shard_map(
        local,
        mesh=mesh,
        in_specs=(
            P("qry", "cent", None, None),
            P("cent", None),
            P("cent", None),
            P("cent", None),
            P("cent", None, None),
            P("cent"),
            P(),
            P("qry", "cent", None, None),
            P("qry", "cent", None),
        ),
        out_specs=(P("qry", "cent", None, None), P("qry", "cent", None)),
        check_vma=False,
    )
```

```python
import functools

import jax
import jax.numpy as jnp
from jax import lax
from jax.experimental import pallas as pl
from jax.experimental.pallas import tpu as pltpu
from jax.sharding import PartitionSpec as P

TOPK = 100
NEG = -1e30
EPS = 1e-6
LOW = float("-inf")
TB = 16
CHUNK = 512
UNIT = 4
MESH = pl.DeviceIdType.MESH
CENT_AXES = (4, 4, 2)
HOPS = (
    (1, 0), (0, 1), (3, 0), (0, 3), (1, 1), (3, 3), (1, 3), (3, 1),
    (2, 0), (0, 2), (2, 1), (1, 2), (2, 3), (3, 2), (2, 2),
)
PART = 112


def place_of(me):
    wide, deep, cores = CENT_AXES
    return lax.div(me, deep * cores), lax.rem(lax.div(me, cores), deep), lax.rem(me, cores)


def peer_of(me, i, sign):
    wide, deep, cores = CENT_AXES
    x, y, core = place_of(me)
    many = len(HOPS)
    j, other = lax.rem(i - 1, many), lax.div(i - 1, many)
    code = 0
    for t, (dx, dy) in enumerate(HOPS):
        code = code + jnp.where(j == t, dx * deep + dy, 0)
    last = i == cores * many + 1
    code = jnp.where(last, 0, code)
    other = jnp.where(last, 1, other)
    dx, dy = lax.div(code, deep), lax.rem(code, deep)
    if sign < 0:
        dx, dy = wide - dx, deep - dy
    x, y, core = lax.rem(x + dx, wide), lax.rem(y + dy, deep), lax.rem(core + other, cores)
    return (x * deep + y) * cores + core


def fetch_kernel(
    tokens, cent_hbm, wanted, own, lengths, packed_hbm, buckets, tab, resid_hbm, qcols, order,
    packed, stage, cent, mid, asked, asked_s, sbuf, qall, qwide, spread, resid, order_s,
    packed_sem, stage_sem, asked_sem, order_sem, own_sem, resid_sem, off_send, off_recv, row_send, row_recv,
    q_send, q_recv, q_row_send, q_row_recv, pair_send, pair_recv, blk_send, blk_recv, half_recv, z_send, left_recv, right_recv, far_recv,
):
    me, z = lax.axis_index("cent"), lax.axis_index("qry")
    n, nz = lax.axis_size("cent"), lax.axis_size("qry")
    wide, deep, cores = CENT_AXES
    line_size = deep * cores
    mx, my, core = place_of(me)
    mr = lax.rem(me, line_size)
    right, far, left = lax.rem(z + 1, nz), lax.rem(z + 2, nz), lax.rem(z + 3, nz)
    rows = tab.shape[2]
    part = sbuf.shape[1] - rows
    pieces = stage_sem.shape[0]
    depth = stage.shape[0] // pieces
    passages = packed.shape[0]
    ptok = packed.shape[2]

    loads = [
        pltpu.make_async_copy(
            cent_hbm.at[i * depth : (i + 1) * depth], stage.at[i * depth : (i + 1) * depth], stage_sem.at[i]
        )
        for i in range(pieces)
    ]
    for load in loads:
        load.start()

    load_packed = pltpu.make_async_copy(packed_hbm, packed, packed_sem)
    load_packed.start()

    def in_row(i):
        return mx * line_size + lax.rem(mr + i, line_size)

    def in_column(i):
        return lax.rem(mx + i, wide) * line_size + mr

    barrier = pltpu.get_barrier_semaphore()
    for i in range(1, line_size):
        pl.semaphore_signal(barrier, inc=1, device_id=(in_row(i), z), device_id_type=MESH)
    for i in range(1, wide):
        pl.semaphore_signal(barrier, inc=1, device_id=(in_column(i), z), device_id_type=MESH)
    for side in (left, right, far):
        pl.semaphore_signal(barrier, inc=1, device_id=(me, side), device_id_type=MESH)

    across = jnp.broadcast_to(lengths[...], (passages, passages))
    down = across.T
    line = lax.broadcasted_iota(jnp.int32, (passages, passages), 0)
    lane = lax.broadcasted_iota(jnp.int32, (passages, passages), 1)
    ahead = (down > across) | ((down == across) & (line < lane))
    rank = jnp.sum(ahead.astype(jnp.int32), axis=0, keepdims=True)
    hit = jnp.broadcast_to(rank, (passages, passages)).T == lane
    order[0:1, :] = jnp.sum(jnp.where(hit, line, 0), axis=0, keepdims=True)
    order[1:2, :] = jnp.sum(jnp.where(hit, down, 0), axis=0, keepdims=True)
    order[2:8, :] = jnp.zeros((6, passages), jnp.int32)
    to_order = pltpu.make_async_copy(order, order_s, order_sem)
    to_order.start()
    for b in range(4):
        spread[b] = jnp.broadcast_to(buckets[b : b + 1, :], (ptok, 128)).T

    def widen(first, last):
        for i in range(first, last):
            loads[i].wait()

            @pl.loop(0, depth // 512)
            def _(j):
                at = pl.ds(pl.multiple_of(i * depth + j * 512, 512), 512)
                cent[at, :] = stage[at, :].astype(jnp.float32)

    widen(0, pieces // 2)
    pl.semaphore_wait(barrier, line_size + wide - 2 + 3)

    def remote(src, dst, send, recv, peer):
        return pltpu.make_async_remote_copy(
            src_ref=src, dst_ref=dst, send_sem=send, recv_sem=recv, device_id=(peer, z), device_id_type=MESH
        )

    for i in range(1, line_size):
        remote(wanted.at[lax.rem(mr + i, line_size)], mid.at[mr], off_send, off_recv, in_row(i)).start()
    for i in range(1, wide):
        remote(own, qall.at[mx, my, core], q_send, q_recv, in_column(i)).start()
    mid[mr] = wanted[mr]
    qall[mx, my, core] = own[...]
    widen(pieces // 2, pieces)
    to_order.wait()
    load_packed.wait()
    first = remote(
        wanted.at[pl.ds(0, line_size - 1)], mid.at[pl.ds(0, line_size - 1)], off_send, off_recv, in_row(1)
    )
    first.wait_recv()
    for i in range(1, wide):
        remote(mid.at[:, lax.rem(mx + i, wide)], asked.at[mx], row_send, row_recv, in_column(i)).start()
    asked[mx] = mid[:, mx]
    remote(qall.at[pl.ds(0, wide - 1), 0, 0], qall.at[pl.ds(0, wide - 1), 0, 0], q_send, q_recv, in_column(1)).wait_recv()
    for i in range(1, deep):
        peer = (mx * deep + lax.rem(my + i, deep)) * cores + core
        remote(qall.at[:, my, core], qall.at[:, my, core], q_row_send, q_row_recv, peer).start()
    second = remote(
        asked.at[pl.ds(0, wide - 1)], asked.at[pl.ds(0, wide - 1)], row_send, row_recv, in_column(1)
    )
    second.wait_recv()
    to_scalar = pltpu.make_async_copy(asked, asked_s, asked_sem)
    to_scalar.start()
    to_scalar.wait()

    sub = lax.broadcasted_iota(jnp.int32, (16, 128), 0)

    def pull(i, peer, line, start, count):
        px, pr = lax.div(peer, line_size), lax.rem(peer, line_size)
        for r in range(0, count, 16):
            tile = jnp.broadcast_to(cent[pl.ds(asked_s[px, pr, line, r], 1), :], (16, 128))
            for k in range(1, 16):
                value = jnp.broadcast_to(cent[pl.ds(asked_s[px, pr, line, r + k], 1), :], (16, 128))
                tile = jnp.where(sub == k, value, tile)
            sbuf[i, start + r : start + r + 16, :] = tile.astype(jnp.bfloat16)

    def block_copy(i, peer):
        return remote(sbuf.at[i, pl.ds(0, rows)], tab.at[me, z], blk_send, blk_recv.at[i], peer)

    pull(0, me, 0, 0, rows)
    keep_own = pltpu.make_async_copy(sbuf.at[0, pl.ds(0, rows)], tab.at[me, z], own_sem.at[0])
    keep_own.start()

    @pl.loop(1, n)
    def _(i):
        peer = peer_of(me, i, 1)
        pull(i, peer, 0, 0, rows)
        block_copy(i, peer).start()

    def along(ref, side, recv):
        return pltpu.make_async_remote_copy(
            src_ref=ref, dst_ref=ref, send_sem=z_send, recv_sem=recv, device_id=(me, side), device_id_type=MESH,
        )

    def forward(owner):
        along(tab.at[owner, z], right, left_recv).start()
        along(tab.at[owner, z], left, right_recv).start()
        if part < rows:
            along(tab.at[owner, z, pl.ds(part, rows - part)], far, far_recv).start()

    def decode(i):
        words = packed[order_s[0, i]]
        digits = jnp.concatenate([(words >> (2 * k)) & 3 for k in range(8)], axis=0)
        low = jnp.where(digits == 0, spread[0], spread[1])
        high = jnp.where(digits == 2, spread[2], spread[3])
        value = jnp.where(digits < 2, low, high)
        resid[lax.div(i, 8), pl.ds(lax.rem(i, 8), ptok, stride=8), :] = value.T

    def extras(k, peer):
        for j in range(passages // n):
            decode(k * (passages // n) + j)
        pull(k, peer, 1, rows, part)

    def save(g):
        return pltpu.make_async_copy(resid.at[g], resid_hbm.at[g], resid_sem)

    def bulk(ref, send, recv):
        return pltpu.make_async_remote_copy(
            src_ref=ref, dst_ref=ref, send_sem=send, recv_sem=recv, device_id=(me, right), device_id_type=MESH,
        )

    keep_own.wait()
    forward(me)
    extras(0, me)
    keep_half = pltpu.make_async_copy(sbuf.at[0, pl.ds(rows, part)], tab.at[me, far, pl.ds(0, part)], own_sem.at[1])
    keep_half.start()

    def relay(k):
        peer = peer_of(me, k, 1)
        block_copy(k, peer).wait_recv()
        forward(peer_of(me, k, -1))
        extras(k, peer)
        remote(
            sbuf.at[k, pl.ds(rows, part)], tab.at[me, far, pl.ds(0, part)], blk_send, half_recv, peer
        ).start()

        @pl.when(lax.rem(k, 2) == 1)
        def _():
            save(lax.div(k, 2)).start()

    per = own.shape[0]
    queries = qcols.shape[1] // tokens

    @pl.loop(1, n // 2)
    def _(k):
        relay(k)

    bulk(qall.at[pl.ds(0, wide), pl.ds(0, deep - 1), 0], q_row_send, q_row_recv).wait_recv()
    pair = remote(qall.at[:, :, core], qall.at[:, :, core], pair_send, pair_recv, me + 1 - 2 * core)
    pair.start()

    @pl.loop(n // 2, n // 4 * 3)
    def _(k):
        relay(k)

    pair.wait()

    @pl.loop(0, wide)
    def _(i):
        for y in range(deep):
            for c in range(cores):
                at = i * (line_size * per) + (y * cores + c) * per
                qwide[pl.ds(pl.multiple_of(at, per), per), :] = qall[i, y, c].astype(jnp.float32)

    for t in range(tokens):
        tile = qwide[pl.ds(t, queries, stride=tokens), :]
        qcols[:, t * queries : (t + 1) * queries] = tile.T.astype(jnp.bfloat16)

    @pl.loop(n // 4 * 3, n)
    def _(k):
        relay(k)

    bulk(tab.at[pl.ds(0, n // nz)], z_send, left_recv).wait_recv()
    bulk(tab.at[pl.ds(0, n // nz)], z_send, right_recv).wait_recv()
    if part < rows:
        bulk(tab.at[pl.ds(0, n), 0, pl.ds(part, rows - part)], z_send, far_recv).wait_recv()
    bulk(sbuf.at[pl.ds(0, n - 1), pl.ds(rows, part)], z_send, half_recv).wait_recv()
    keep_half.wait()
    pltpu.make_async_copy(resid, resid_hbm, resid_sem).wait()
    first.wait_send()
    second.wait_send()
    bulk(qall.at[pl.ds(0, wide - 1), 0, 0], q_send, q_recv).wait_send()
    bulk(qall.at[pl.ds(0, wide), pl.ds(0, deep - 1), 0], q_row_send, q_row_recv).wait_send()
    bulk(sbuf.at[pl.ds(0, n - 1)], blk_send, q_recv).wait_send()
    bulk(tab.at[pl.ds(0, 2 * n // nz)], z_send, q_recv).wait_send()
    if part < rows:
        bulk(tab.at[pl.ds(0, n), 0, pl.ds(part, rows - part)], z_send, q_recv).wait_send()


def fetch(centroids, wanted, own, lengths, packed, buckets, tokens):
    n, nz = lax.axis_size("cent"), lax.axis_size("qry")
    wide, deep, cores = CENT_AXES
    rows = wanted.shape[3]
    part = PART
    passages, _, ptok = packed.shape
    vmem = pl.BlockSpec(memory_space=pltpu.VMEM)
    hbm = pl.BlockSpec(memory_space=pl.ANY)
    dma = pltpu.SemaphoreType.DMA
    groups = passages // 8
    return pl.pallas_call(
        functools.partial(fetch_kernel, tokens),
        out_shape=(
            jax.ShapeDtypeStruct((n, nz, rows, 128), jnp.bfloat16),
            jax.ShapeDtypeStruct((groups, 8 * ptok, 128), jnp.float32),
            jax.ShapeDtypeStruct((128, n * own.shape[0]), jnp.bfloat16),
            jax.ShapeDtypeStruct((8, passages), jnp.int32),
        ),
        in_specs=[hbm, vmem, vmem, vmem, hbm, vmem],
        out_specs=(hbm, hbm, vmem, vmem),
        scratch_shapes=[
            pltpu.VMEM(packed.shape, jnp.int32),
            pltpu.VMEM(centroids.shape, jnp.bfloat16),
            pltpu.VMEM(centroids.shape, jnp.float32),
            pltpu.VMEM((deep * cores, wide, 2, rows), jnp.int32),
            pltpu.VMEM((wide, deep * cores, 2, rows), jnp.int32),
            pltpu.SMEM((wide, deep * cores, 2, rows), jnp.int32),
            pltpu.VMEM((n, rows + part, 128), jnp.bfloat16),
            pltpu.VMEM(CENT_AXES + own.shape, jnp.bfloat16),
            pltpu.VMEM((n * own.shape[0], 128), jnp.float32),
            pltpu.VMEM((4, 128, ptok), jnp.float32),
            pltpu.VMEM((groups, 8 * ptok, 128), jnp.float32),
            pltpu.SMEM((8, passages), jnp.int32),
            dma, dma((8,)), dma, dma, dma((2,)), dma, dma, dma, dma, dma,
            dma, dma, dma, dma, dma, dma, dma, dma((n,)), dma, dma, dma, dma, dma,
        ],
        compiler_params=pltpu.CompilerParams(
            collective_id=0, has_side_effects=True, vmem_limit_bytes=58 * 2**20
        ),
    )(centroids, wanted, own, lengths, packed, buckets)


def score_kernel(
    refs, order, order_ref, table_hbm, resid_hbm, q_hbm, cand_ref, live_ref,
    out_ref, stage, tab, resid, q_ref, first, acc, scores, len_ref, blk_g, blk_b, stage_sem, resid_sem, q_sem,
):
    passages = order.shape[1]
    groups = passages // 8
    columns = q_ref.shape[1]
    slots, queries = cand_ref.shape
    ptok = resid_hbm.shape[1] // 8
    rows = TB * 8
    pieces = stage_sem.shape[0]
    depth = stage.shape[0] // pieces

    def load(i):
        return pltpu.make_async_copy(
            table_hbm.at[pl.ds(pl.multiple_of(i * depth, depth), depth)],
            stage.at[lax.rem(i, 2)], stage_sem.at[lax.rem(i, 2)],
        )

    loads = [
        pltpu.make_async_copy(
            table_hbm.at[i * depth : (i + 1) * depth], stage.at[i * depth : (i + 1) * depth], stage_sem.at[i]
        )
        for i in range(pieces)
    ]
    for load in loads:
        load.start()
    load_q = pltpu.make_async_copy(q_hbm, q_ref, q_sem)
    load_q.start()

    def load_resid(g):
        return pltpu.make_async_copy(resid_hbm.at[g], resid.at[g], resid_sem.at[g])

    @pl.loop(0, groups)
    def _(g):
        load_resid(g).start()

    acc[...] = jnp.full(acc.shape, LOW, jnp.float32)
    spread = jnp.broadcast_to(order_ref[1:2, :], (passages, passages)).T
    len_ref[...] = spread.reshape(groups, 8, 128)

    def add_group(g, n):
        count = lax.div(order[1, g * 8] + (TB - 1), TB)

        def add(b, m):
            blk_g[m] = g
            blk_b[m] = b
            return m + 1

        return lax.fori_loop(0, count, add, n)

    total = lax.fori_loop(0, groups, add_group, 0)
    for extra in range(UNIT - 1):
        blk_g[total + extra] = blk_g[total - 1]
        blk_b[total + extra] = blk_b[total - 1]
    steps = lax.div(total + (UNIT - 1), UNIT)

    for i, load in enumerate(loads):
        load.wait()

        @pl.loop(0, depth // 512)
        def _(j):
            at = pl.ds(pl.multiple_of(i * depth + j * 512, 512), 512)
            tab[at, :] = stage[at, :].astype(jnp.float32)

    load_q.wait()

    def arrive(first_group, last_group):
        @pl.loop(first_group, last_group + 1)
        def _(g):
            load_resid(g).wait()

    arrive(0, blk_g[UNIT - 1])

    def embed_one(u, i, head):
        g, b = blk_g[i], blk_b[i]
        where = [order[0, g * 8 + p] * ptok + b * TB for p in range(8)]
        sub = lax.broadcasted_iota(jnp.int32, (8, 128), 0)
        tiles = []
        for t in range(TB):
            tile = jnp.broadcast_to(tab[pl.ds(refs[where[0] + t], 1), :], (8, 128))
            for p in range(1, 8):
                tile = jnp.where(sub == p, jnp.broadcast_to(tab[pl.ds(refs[where[p] + t], 1), :], (8, 128)), tile)
            tiles.append(tile)
        got = jnp.concatenate(tiles, axis=0)
        start = pl.multiple_of(b * rows, rows)
        summed = got + resid[g, pl.ds(start, rows), :]
        norm = jnp.sum(summed * summed, axis=1, keepdims=True)
        unit = (summed * lax.rsqrt(norm + EPS)).reshape(TB, 8, 128)
        head = jnp.where(b == 0, unit[0], head)
        token = b * TB + lax.broadcasted_iota(jnp.int32, (TB, 8, 128), 0)
        unit = jnp.where(token < len_ref[g][None], unit, head[None])
        return unit.reshape(rows, 128).astype(jnp.bfloat16), head

    def embed(s):
        head = first[...]
        units = []
        for u in range(UNIT):
            unit, head = embed_one(u, s * UNIT + u, head)
            units.append(unit)
        first[...] = head
        return jnp.concatenate(units, axis=0)

    def step(s, unit):
        later = jnp.minimum(s + 1, steps - 1)
        arrive(blk_g[s * UNIT + UNIT - 1] + 1, blk_g[later * UNIT + UNIT - 1])
        group = [blk_g[s * UNIT + u] for u in range(UNIT)]
        head = first[...]
        following = []
        parts = columns // CHUNK // UNIT
        for part, c in enumerate(range(0, columns, CHUNK)):
            if part % parts == 0:
                u = part // parts
                block, head = embed_one(u, later * UNIT + u, head)
                following.append(block)
            sim = jnp.dot(unit, q_ref[:, c : c + CHUNK], preferred_element_type=jnp.float32)
            best = jnp.max(sim.reshape(UNIT, TB, 8, CHUNK), axis=1)
            for u in range(UNIT):
                acc[group[u], :, c : c + CHUNK] = jnp.maximum(acc[group[u], :, c : c + CHUNK], best[u])
        first[...] = head
        return jnp.concatenate(following, axis=0)

    lax.fori_loop(0, steps, step, embed(0))

    @pl.loop(0, groups)
    def _(g):
        total_sum = acc[g, :, 0:queries]
        for t in range(1, columns // queries):
            total_sum = total_sum + acc[g, :, t * queries : (t + 1) * queries]
        scores[pl.ds(pl.multiple_of(g * 8, 8), 8), :] = total_sum

    cand = cand_ref[...]

    def pick(r, picked):
        return jnp.where(cand == order[0, r], scores[pl.ds(r, 1), :], picked)

    picked = lax.fori_loop(0, passages, pick, jnp.zeros((slots, queries), jnp.float32), unroll=8)
    place = lax.broadcasted_iota(jnp.int32, (slots, queries), 0)
    values = jnp.where(place < live_ref[...], picked, NEG)
    place_out = lax.broadcasted_iota(jnp.int32, (16, queries), 0)
    tops = jnp.zeros((16, queries), jnp.float32)
    for k in range(slots // 4):
        top = jnp.max(values, axis=0, keepdims=True)
        tops = jnp.where(place_out == k, top, tops)
        at = jnp.min(jnp.where(values == top, place, slots), axis=0, keepdims=True)
        values = jnp.where(place == at, LOW, values)
    padded = jnp.concatenate([tops, jnp.zeros((128 - 16, queries), jnp.float32)], axis=0)
    out_ref[...] = padded.T


def score(table, refs, order, resid, qcols, cand, live):
    groups = resid.shape[0]
    passages = order.shape[1]
    queries, slots = cand.shape
    vmem = pl.BlockSpec(memory_space=pltpu.VMEM)
    smem = pl.BlockSpec(memory_space=pltpu.SMEM)
    hbm = pl.BlockSpec(memory_space=pl.ANY)
    blocks = resid.shape[0] * resid.shape[1] // (8 * TB) + UNIT
    return pl.pallas_call(
        score_kernel,
        out_shape=jax.ShapeDtypeStruct((queries, 128), jnp.float32),
        in_specs=[smem, smem, vmem, hbm, hbm, hbm, vmem, vmem],
        out_specs=vmem,
        scratch_shapes=[
            pltpu.VMEM(table.shape, jnp.bfloat16),
            pltpu.VMEM((table.shape[0], 128), jnp.float32),
            pltpu.VMEM(resid.shape, jnp.float32),
            pltpu.VMEM(qcols.shape, jnp.bfloat16),
            pltpu.VMEM((8, 128), jnp.float32),
            pltpu.VMEM((groups, 8, qcols.shape[1]), jnp.float32),
            pltpu.VMEM((passages, queries), jnp.float32),
            pltpu.VMEM((groups, 8, 128), jnp.int32),
            pltpu.SMEM((blocks,), jnp.int32),
            pltpu.SMEM((blocks,), jnp.int32),
            pltpu.SemaphoreType.DMA((8,)),
            pltpu.SemaphoreType.DMA((groups,)),
            pltpu.SemaphoreType.DMA,
        ],
        compiler_params=pltpu.CompilerParams(vmem_limit_bytes=56 * 2**20),
    )(refs.reshape(-1), order, order, table, resid, qcols, cand.T, live[None, :])


def swap_kernel(tops, inbox, outbox, mid, row_send, row_recv, send, recv):
    me, z = lax.axis_index("cent"), lax.axis_index("qry")
    wide, deep, cores = CENT_AXES
    line_size = deep * cores
    mx, mr = lax.div(me, line_size), lax.rem(me, line_size)
    per = outbox.shape[2]

    def in_row(i):
        return mx * line_size + lax.rem(mr + i, line_size)

    def in_column(i):
        return lax.rem(mx + i, wide) * line_size + mr

    barrier = pltpu.get_barrier_semaphore()
    for i in range(1, line_size):
        pl.semaphore_signal(barrier, inc=1, device_id=(in_row(i), z), device_id_type=MESH)
    for i in range(1, wide):
        pl.semaphore_signal(barrier, inc=1, device_id=(in_column(i), z), device_id_type=MESH)
    for x in range(wide):
        for r in range(line_size):
            at = (x * line_size + r) * per
            outbox[r, x] = tops[at : at + per, :]
    mid[mr] = outbox[mr]
    pl.semaphore_wait(barrier, line_size + wide - 2)

    def remote(src, dst, send_sem, recv_sem, peer):
        return pltpu.make_async_remote_copy(
            src_ref=src, dst_ref=dst, send_sem=send_sem, recv_sem=recv_sem, device_id=(peer, z), device_id_type=MESH
        )

    for i in range(1, line_size):
        remote(outbox.at[lax.rem(mr + i, line_size)], mid.at[mr], row_send, row_recv, in_row(i)).start()
    most = pl.ds(0, line_size - 1)
    remote(outbox.at[most], mid.at[most], row_send, row_recv, in_row(1)).wait()
    for i in range(1, wide):
        remote(mid.at[:, lax.rem(mx + i, wide)], inbox.at[mx], send, recv, in_column(i)).start()
    inbox[mx] = mid[:, mx]
    most = pl.ds(0, wide - 1)
    remote(inbox.at[most], inbox.at[most], send, recv, in_column(1)).wait()


def swap(tops, per):
    n = lax.axis_size("cent")
    wide, deep, cores = CENT_AXES
    vmem = pl.BlockSpec(memory_space=pltpu.VMEM)
    dma = pltpu.SemaphoreType.DMA
    inbox = pl.pallas_call(
        swap_kernel,
        out_shape=jax.ShapeDtypeStruct((wide, deep * cores, per, 128), jnp.float32),
        in_specs=[vmem],
        out_specs=vmem,
        scratch_shapes=[
            pltpu.VMEM((deep * cores, wide, per, 128), jnp.float32),
            pltpu.VMEM((deep * cores, wide, per, 128), jnp.float32),
            dma, dma, dma, dma,
        ],
        compiler_params=pltpu.CompilerParams(collective_id=1, has_side_effects=True),
    )(tops)
    return inbox.reshape(n, per, 128)


def merge_kernel(inbox, shard_out, best_out):
    n, per = inbox.shape[:2]
    keep = shard_out.shape[0]
    lists = [inbox[:, q, :] for q in range(per)]
    column = jnp.concatenate(lists, axis=0)
    across = column.T
    width = per * n
    row = across[0:16, :]
    for q in range(per):
        shard_out[:, q, :] = row[:keep, q * n : (q + 1) * n]
    lane = lax.broadcasted_iota(jnp.int32, (16, width), 1)
    shard = lax.rem(lane, n)
    place = lax.broadcasted_iota(jnp.int32, (16, width), 0)

    rank = place
    for r in range(1, n):
        near = pltpu.roll(row, r, 1)
        far = pltpu.roll(row, r + width - n, 1)
        wrapped = shard < r
        other = jnp.where(wrapped, far, near)
        for k in range(keep):
            rival = other[k : k + 1, :]
            ahead = (rival > row) | ((rival == row) & ~wrapped)
            rank = rank + ahead.astype(jnp.int32)
    ranks = jnp.concatenate([rank, jnp.zeros((width - 16, width), jnp.int32)], axis=0).T
    target = lax.broadcasted_iota(jnp.int32, (width, 128), 1)
    found = jnp.zeros((width, 128), jnp.float32)
    for k in range(keep):
        found = found + jnp.where(ranks[:, k : k + 1] == target, column[:, k : k + 1], 0.0)
    for q in range(per):
        best = jnp.sum(found[q * n : (q + 1) * n, :], axis=0, keepdims=True)
        best_out[q : q + 1, :] = best[:, :TOPK]


def merge(inbox, keep):
    n, per, _ = inbox.shape
    vmem = pl.BlockSpec(memory_space=pltpu.VMEM)
    return pl.pallas_call(
        merge_kernel,
        out_shape=(
            jax.ShapeDtypeStruct((keep, per, n), jnp.float32),
            jax.ShapeDtypeStruct((per, TOPK), jnp.float32),
        ),
        in_specs=[vmem],
        out_specs=(vmem, vmem),
    )(inbox)


def local(
    queries,
    centroids,
    shard_table,
    token_refs,
    packed_residual_buckets,
    passage_lengths,
    bucket_values,
    candidates,
    live_counts,
):
    n, nz = lax.axis_size("cent"), lax.axis_size("qry")
    per, tokens, width = queries.shape[1:]
    z = lax.axis_index("qry")
    by_owner = shard_table.reshape(n, nz, -1)
    wanted = jnp.concatenate(
        [lax.dynamic_slice_in_dim(by_owner, quarter, 1, 1) for quarter in (z, lax.rem(z + 2, nz))], axis=1
    )
    wanted = jnp.swapaxes(wanted.reshape((CENT_AXES[0], n // CENT_AXES[0]) + wanted.shape[1:]), 0, 1)
    table, resid, qcols, order = fetch(
        centroids, wanted, queries.reshape(per * tokens, width), passage_lengths[None, :], packed_residual_buckets,
        bucket_values, tokens,
    )
    tops = score(table.reshape(-1, width), token_refs, order, resid, qcols, candidates[0, 0], live_counts[0, 0])
    shard_tops, best_scores = merge(swap(tops, per), candidates.shape[3] // 4)
    return (jnp.transpose(shard_tops, (1, 2, 0))[None], best_scores[None])


def solution(mesh):
    return jax.shard_map(
        local,
        mesh=mesh,
        in_specs=(
            P("qry", "cent", None, None),
            P("cent", None),
            P("cent", None),
            P("cent", None),
            P("cent", None, None),
            P("cent"),
            P(),
            P("qry", "cent", None, None),
            P("qry", "cent", None),
        ),
        out_specs=(P("qry", "cent", None, None), P("qry", "cent", None)),
        check_vma=False,
    )
```

```python
import jax
import jax.numpy as jnp
from jax import lax
from jax.experimental import pallas as pl
from jax.experimental.pallas import tpu as pltpu
from jax.sharding import PartitionSpec as P

TOPK = 100
NEG = -1e30
EPS = 1e-6
LOW = float("-inf")
TB = 16
GROUP = 4
TILES = 4
MESH = pl.DeviceIdType.MESH
CENT_AXES = (4, 4, 2)
HOPS = (
    (1, 0), (0, 1), (3, 0), (0, 3), (1, 1), (3, 3), (1, 3), (3, 1),
    (2, 0), (0, 2), (2, 1), (1, 2), (2, 3), (3, 2), (2, 2),
)
PART = 128


def place_of(me):
    wide, deep, cores = CENT_AXES
    return lax.div(me, deep * cores), lax.rem(lax.div(me, cores), deep), lax.rem(me, cores)


def peer_of(me, i, sign):
    wide, deep, cores = CENT_AXES
    x, y, core = place_of(me)
    many = len(HOPS)
    j, other = lax.rem(i - 1, many), lax.div(i - 1, many)
    code = 0
    for t, (dx, dy) in enumerate(HOPS):
        code = code + jnp.where(j == t, dx * deep + dy, 0)
    last = i == cores * many + 1
    code = jnp.where(last, 0, code)
    other = jnp.where(last, 1, other)
    dx, dy = lax.div(code, deep), lax.rem(code, deep)
    if sign < 0:
        dx, dy = wide - dx, deep - dy
    x, y, core = lax.rem(x + dx, wide), lax.rem(y + dy, deep), lax.rem(core + other, cores)
    return (x * deep + y) * cores + core


def fetch_kernel(
    cent_hbm, wanted, own, lengths, packed_hbm, buckets, cand, live, tab, resid_hbm, qall, order, members, place,
    packed, stage, cent, mid, asked, asked_s, sbuf, spread, resid, spots, order_s,
    packed_sem, stage_sem, asked_sem, order_sem, own_sem, resid_sem, off_send, off_recv, row_send, row_recv,
    q_send, q_recv, q_row_send, q_row_recv, pair_send, pair_recv, blk_send, blk_recv, half_recv, z_send, left_recv, right_recv,
):
    me, z = lax.axis_index("cent"), lax.axis_index("qry")
    n, nz = lax.axis_size("cent"), lax.axis_size("qry")
    wide, deep, cores = CENT_AXES
    line_size = deep * cores
    mx, my, core = place_of(me)
    mr = lax.rem(me, line_size)
    right, far, left = lax.rem(z + 1, nz), lax.rem(z + 2, nz), lax.rem(z + 3, nz)
    rows = tab.shape[2]
    part = sbuf.shape[1] - rows
    slots, queries = cand.shape
    pieces = stage_sem.shape[0]
    depth = stage.shape[0] // pieces
    passages = packed.shape[0]
    ptok = packed.shape[2]

    loads = [
        pltpu.make_async_copy(
            cent_hbm.at[i * depth : (i + 1) * depth], stage.at[i * depth : (i + 1) * depth], stage_sem.at[i]
        )
        for i in range(pieces)
    ]
    for load in loads:
        load.start()

    load_packed = pltpu.make_async_copy(packed_hbm, packed, packed_sem)
    load_packed.start()

    def in_row(i):
        return mx * line_size + lax.rem(mr + i, line_size)

    def in_column(i):
        return lax.rem(mx + i, wide) * line_size + mr

    barrier = pltpu.get_barrier_semaphore()
    for i in range(1, line_size):
        pl.semaphore_signal(barrier, inc=1, device_id=(in_row(i), z), device_id_type=MESH)
    for i in range(1, wide):
        pl.semaphore_signal(barrier, inc=1, device_id=(in_column(i), z), device_id_type=MESH)
    for side in (left, right):
        pl.semaphore_signal(barrier, inc=1, device_id=(me, side), device_id_type=MESH)

    across = jnp.broadcast_to(lengths[...], (passages, passages))
    down = across.T
    line = lax.broadcasted_iota(jnp.int32, (passages, passages), 0)
    lane = lax.broadcasted_iota(jnp.int32, (passages, passages), 1)
    ahead = (down > across) | ((down == across) & (line < lane))
    rank = jnp.sum(ahead.astype(jnp.int32), axis=0, keepdims=True)
    hit = jnp.broadcast_to(rank, (passages, passages)).T == lane
    order[0:1, :] = jnp.sum(jnp.where(hit, line, 0), axis=0, keepdims=True)
    order[1:2, :] = jnp.sum(jnp.where(hit, down, 0), axis=0, keepdims=True)
    lens = order[1:2, :]
    owner_of = jnp.broadcast_to(order[0:1, :], (passages, queries)).T

    def mark(slot, need):
        hit = (owner_of == cand[pl.ds(slot, 1), :]) & (live[...] > slot)
        return jnp.where(hit, 1.0, need)

    need = lax.fori_loop(0, slots, mark, jnp.zeros((passages, queries), jnp.float32), unroll=4)
    flags = need.astype(jnp.bfloat16)
    before = (line < lane).astype(jnp.bfloat16)
    spot = jnp.dot(flags, before, preferred_element_type=jnp.float32)
    place[...] = jnp.where(need > 0, spot, 0.0).astype(jnp.int32)
    spots[...] = jnp.where(need > 0, spot, -1.0)
    across_lanes = (((1,), (1,)), ((), ()))
    counts = lax.dot_general(
        jnp.ones((8, queries), jnp.bfloat16), flags, across_lanes, preferred_element_type=jnp.float32
    )[0:1]
    order[2:3, :] = counts.astype(jnp.int32)
    order[3:4, :] = jnp.broadcast_to(jnp.max(counts, axis=1, keepdims=True), (1, passages)).astype(jnp.int32)
    heads = jnp.where((lane % GROUP == 0) & (lens > line * TB), 1.0, 0.0).astype(jnp.bfloat16)
    order[4:5, :] = lax.dot_general(
        jnp.ones((8, passages), jnp.bfloat16), heads, across_lanes, preferred_element_type=jnp.float32
    )[0:1].astype(jnp.int32)
    most = TILES * (256 * queries // (own.shape[0] * n))
    number = lax.broadcasted_iota(jnp.int32, (8, queries), 1).astype(jnp.float32).astype(jnp.bfloat16)
    index = lax.broadcasted_iota(jnp.int32, (queries, queries), 0).astype(jnp.float32)
    over = jnp.broadcast_to(counts, (8, passages)) > most
    over_flags = jnp.where(over, 1.0, 0.0)
    over_spot = jnp.dot(over_flags.astype(jnp.bfloat16), before, preferred_element_type=jnp.float32)
    over_hit = jnp.where(jnp.where(over, over_spot, -1.0)[0:1] == index, 1.0, 0.0).astype(jnp.bfloat16)
    order[5:6, :] = lax.dot_general(number, over_hit, across_lanes, preferred_element_type=jnp.float32)[0:1].astype(
        jnp.int32
    )
    over_count = jnp.sum(over_flags[0:1], axis=1, keepdims=True)
    order[6:7, :] = jnp.broadcast_to(over_count, (1, passages)).astype(jnp.int32)
    order[7:8, :] = jnp.zeros((1, passages), jnp.int32)
    to_order = pltpu.make_async_copy(order, order_s, order_sem)
    to_order.start()
    for b in range(4):
        spread[b] = jnp.broadcast_to(buckets[b : b + 1, :], (ptok, 128)).T

    def widen(first, last):
        for i in range(first, last):
            loads[i].wait()

            @pl.loop(0, depth // 512)
            def _(j):
                at = pl.ds(pl.multiple_of(i * depth + j * 512, 512), 512)
                cent[at, :] = stage[at, :].astype(jnp.float32)

    widen(0, pieces // 2)
    pl.semaphore_wait(barrier, line_size + wide)

    def remote(src, dst, send, recv, peer):
        return pltpu.make_async_remote_copy(
            src_ref=src, dst_ref=dst, send_sem=send, recv_sem=recv, device_id=(peer, z), device_id_type=MESH
        )

    for i in range(1, line_size):
        remote(wanted.at[lax.rem(mr + i, line_size)], mid.at[mr], off_send, off_recv, in_row(i)).start()
    for i in range(1, wide):
        remote(own, qall.at[mx, my, core], q_send, q_recv, in_column(i)).start()
    mid[mr] = wanted[mr]
    keep_queries = pltpu.make_async_copy(own, qall.at[mx, my, core], own_sem.at[2])
    keep_queries.start()
    widen(pieces // 2, pieces)
    to_order.wait()
    load_packed.wait()
    first = remote(
        wanted.at[pl.ds(0, line_size - 1)], mid.at[pl.ds(0, line_size - 1)], off_send, off_recv, in_row(1)
    )
    first.wait_recv()
    for i in range(1, wide):
        remote(mid.at[:, lax.rem(mx + i, wide)], asked.at[mx], row_send, row_recv, in_column(i)).start()
    asked[mx] = mid[:, mx]
    remote(qall.at[pl.ds(0, wide - 1), 0, 0], qall.at[pl.ds(0, wide - 1), 0, 0], q_send, q_recv, in_column(1)).wait_recv()
    keep_queries.wait()
    for i in range(1, deep):
        peer = (mx * deep + lax.rem(my + i, deep)) * cores + core
        remote(qall.at[:, my, core], qall.at[:, my, core], q_row_send, q_row_recv, peer).start()
    second = remote(
        asked.at[pl.ds(0, wide - 1)], asked.at[pl.ds(0, wide - 1)], row_send, row_recv, in_column(1)
    )
    second.wait_recv()
    to_scalar = pltpu.make_async_copy(asked, asked_s, asked_sem)
    to_scalar.start()
    to_scalar.wait()

    sub = lax.broadcasted_iota(jnp.int32, (16, 128), 0)

    def pull(i, peer, line, start, count):
        px, pr = lax.div(peer, line_size), lax.rem(peer, line_size)
        for r in range(0, count, 16):
            tile = jnp.broadcast_to(cent[pl.ds(asked_s[px, pr, line, r], 1), :], (16, 128))
            for k in range(1, 16):
                value = jnp.broadcast_to(cent[pl.ds(asked_s[px, pr, line, r + k], 1), :], (16, 128))
                tile = jnp.where(sub == k, value, tile)
            sbuf[i, start + r : start + r + 16, :] = tile.astype(jnp.bfloat16)

    def block_copy(i, peer):
        return remote(sbuf.at[i, pl.ds(0, rows)], tab.at[me, z], blk_send, blk_recv.at[i], peer)

    pull(0, me, 0, 0, rows)
    keep_own = pltpu.make_async_copy(sbuf.at[0, pl.ds(0, rows)], tab.at[me, z], own_sem.at[0])
    keep_own.start()

    @pl.loop(1, n)
    def _(i):
        peer = peer_of(me, i, 1)
        pull(i, peer, 0, 0, rows)
        block_copy(i, peer).start()

    def along(ref, side, recv):
        return pltpu.make_async_remote_copy(
            src_ref=ref, dst_ref=ref, send_sem=z_send, recv_sem=recv, device_id=(me, side), device_id_type=MESH,
        )

    def forward(owner):
        along(tab.at[owner, z], right, left_recv).start()
        along(tab.at[owner, z], left, right_recv).start()

    def decode(i):
        words = packed[order_s[0, i]]
        digits = jnp.concatenate([(words >> (2 * k)) & 3 for k in range(8)], axis=0)
        low = jnp.where(digits == 0, spread[0], spread[1])
        high = jnp.where(digits == 2, spread[2], spread[3])
        value = jnp.where(digits < 2, low, high)
        resid[i] = value.T

    def enlist(i):
        hit = jnp.where(spots[pl.ds(i, 1), :] == index, 1.0, 0.0).astype(jnp.bfloat16)
        listed = lax.dot_general(number, hit, across_lanes, preferred_element_type=jnp.float32)
        members[pl.ds(i, 1), :] = listed[0:1].astype(jnp.int32)

    def extras(k, peer):
        for j in range(passages // n):
            decode(k * (passages // n) + j)
            enlist(k * (passages // n) + j)
        pull(k, peer, 1, rows, part)

    def save(g):
        at = pl.ds(g * 8, 8)
        return pltpu.make_async_copy(resid.at[at], resid_hbm.at[at], resid_sem)

    def bulk(ref, send, recv):
        return pltpu.make_async_remote_copy(
            src_ref=ref, dst_ref=ref, send_sem=send, recv_sem=recv, device_id=(me, right), device_id_type=MESH,
        )

    keep_own.wait()
    forward(me)
    extras(0, me)
    keep_half = pltpu.make_async_copy(sbuf.at[0, pl.ds(rows, part)], tab.at[me, far, pl.ds(0, part)], own_sem.at[1])
    keep_half.start()

    def relay(k):
        peer = peer_of(me, k, 1)
        block_copy(k, peer).wait_recv()
        forward(peer_of(me, k, -1))
        extras(k, peer)
        remote(
            sbuf.at[k, pl.ds(rows, part)], tab.at[me, far, pl.ds(0, part)], blk_send, half_recv, peer
        ).start()

        @pl.when(lax.rem(k, 2) == 1)
        def _():
            save(lax.div(k, 2)).start()

    @pl.loop(1, n // 2)
    def _(k):
        relay(k)

    bulk(qall.at[pl.ds(0, wide), pl.ds(0, deep - 1), 0], q_row_send, q_row_recv).wait_recv()
    pair = remote(qall.at[:, :, core], qall.at[:, :, core], pair_send, pair_recv, me + 1 - 2 * core)
    pair.start()

    @pl.loop(n // 2, n)
    def _(k):
        relay(k)

    pair.wait()
    bulk(tab.at[pl.ds(0, n // nz)], z_send, left_recv).wait_recv()
    bulk(tab.at[pl.ds(0, n // nz)], z_send, right_recv).wait_recv()
    bulk(sbuf.at[pl.ds(0, n - 1), pl.ds(rows, part)], z_send, half_recv).wait_recv()
    keep_half.wait()
    pltpu.make_async_copy(resid, resid_hbm, resid_sem).wait()
    first.wait_send()
    second.wait_send()
    bulk(qall.at[pl.ds(0, wide - 1), 0, 0], q_send, q_recv).wait_send()
    bulk(qall.at[pl.ds(0, wide), pl.ds(0, deep - 1), 0], q_row_send, q_row_recv).wait_send()
    bulk(sbuf.at[pl.ds(0, n - 1)], blk_send, q_recv).wait_send()
    bulk(tab.at[pl.ds(0, 2 * n // nz)], z_send, q_recv).wait_send()


def fetch(centroids, wanted, own, lengths, packed, buckets, cand, live):
    n, nz = lax.axis_size("cent"), lax.axis_size("qry")
    wide, deep, cores = CENT_AXES
    rows = wanted.shape[3]
    part = PART
    passages, _, ptok = packed.shape
    vmem = pl.BlockSpec(memory_space=pltpu.VMEM)
    hbm = pl.BlockSpec(memory_space=pl.ANY)
    dma = pltpu.SemaphoreType.DMA
    queries = cand.shape[1]
    return pl.pallas_call(
        fetch_kernel,
        out_shape=(
            jax.ShapeDtypeStruct((n, nz, rows, 128), jnp.bfloat16),
            jax.ShapeDtypeStruct((passages, ptok, 128), jnp.float32),
            jax.ShapeDtypeStruct(CENT_AXES + own.shape, jnp.bfloat16),
            jax.ShapeDtypeStruct((8, passages), jnp.int32),
            jax.ShapeDtypeStruct((passages, queries), jnp.int32),
            jax.ShapeDtypeStruct((passages, queries), jnp.int32),
        ),
        in_specs=[hbm, vmem, vmem, vmem, hbm, vmem, vmem, vmem],
        out_specs=(hbm, hbm, hbm, vmem, vmem, vmem),
        scratch_shapes=[
            pltpu.VMEM(packed.shape, jnp.int32),
            pltpu.VMEM(centroids.shape, jnp.bfloat16),
            pltpu.VMEM(centroids.shape, jnp.float32),
            pltpu.VMEM((deep * cores, wide, 2, rows), jnp.int32),
            pltpu.VMEM((wide, deep * cores, 2, rows), jnp.int32),
            pltpu.SMEM((wide, deep * cores, 2, rows), jnp.int32),
            pltpu.VMEM((n, rows + part, 128), jnp.bfloat16),
            pltpu.VMEM((4, 128, ptok), jnp.float32),
            pltpu.VMEM((passages, ptok, 128), jnp.float32),
            pltpu.VMEM((passages, queries), jnp.float32),
            pltpu.SMEM((8, passages), jnp.int32),
            dma, dma((8,)), dma, dma, dma((3,)), dma, dma, dma, dma, dma,
            dma, dma, dma, dma, dma, dma, dma, dma((n,)), dma, dma, dma, dma,
        ],
        compiler_params=pltpu.CompilerParams(
            collective_id=0, has_side_effects=True, vmem_limit_bytes=58 * 2**20
        ),
    )(centroids, wanted, own, lengths, packed, buckets, cand, live)


def score_kernel(
    order, refs_hbm, members_hbm, order_ref, place_ref, table_hbm, resid_hbm, q_hbm, cand_ref, live_ref,
    out_ref, refs, members, stage, tab, resid, q_ref, embeds, best, scores, refs_sem, members_sem, stage_sem, resid_sem, q_sem,
):
    passages = order.shape[1]
    groups = passages // GROUP
    slots, queries = cand_ref.shape
    ptok = resid_hbm.shape[1]
    tokens = q_hbm.shape[0] // queries
    wide = 256 // tokens
    pieces = stage_sem.shape[0]
    depth = stage.shape[0] // pieces
    loads = [
        pltpu.make_async_copy(
            table_hbm.at[i * depth : (i + 1) * depth], stage.at[i * depth : (i + 1) * depth], stage_sem.at[i]
        )
        for i in range(pieces)
    ]
    for load in loads:
        load.start()
    load_refs = pltpu.make_async_copy(refs_hbm, refs, refs_sem)
    load_refs.start()

    def load_resid(g):
        at = pl.ds(g * GROUP, GROUP)
        return pltpu.make_async_copy(resid_hbm.at[at], resid.at[at], resid_sem.at[g])

    load_members = pltpu.make_async_copy(members_hbm, members, members_sem)
    load_members.start()

    @pl.loop(0, groups)
    def _(g):
        load_resid(g).start()

    load_q = pltpu.make_async_copy(q_hbm, q_ref, q_sem)
    load_q.start()

    ends = [order[4, c] for c in range(ptok // TB)]

    for i, load in enumerate(loads):
        load.wait()

        @pl.loop(0, depth // 512)
        def _(j):
            at = pl.ds(pl.multiple_of(i * depth + j * 512, 512), 512)
            tab[at, :] = stage[at, :].astype(jnp.float32)

    load_refs.wait()
    load_resid(0).wait()
    sub = lax.broadcasted_iota(jnp.int32, (8, 128), 0)

    def embed(r, rows):
        source = order[0, r] * ptok
        tiles = []
        for t in range(0, rows, 8):
            tile = jnp.broadcast_to(tab[pl.ds(refs[source + t], 1), :], (8, 128))
            for p in range(1, 8):
                row = jnp.broadcast_to(tab[pl.ds(refs[source + t + p], 1), :], (8, 128))
                tile = jnp.where(sub == p, row, tile)
            tiles.append(tile)
        summed = jnp.concatenate(tiles, axis=0) + resid[r, 0:rows, :]
        norm = jnp.sum(summed * summed, axis=1, keepdims=True)
        unit = summed * lax.rsqrt(norm + EPS)
        line = lax.broadcasted_iota(jnp.int32, unit.shape, 0)
        unit = jnp.where(line < order[1, r], unit, unit[0:1]).astype(jnp.bfloat16)
        embeds[r, 0:rows, :] = unit
        return unit

    def weights(r, k):
        parts = []
        for j in range(wide):
            at = pl.multiple_of(members[r, k * wide + j] * tokens, tokens)
            parts.append(q_ref[pl.ds(at, tokens), :])
        return jnp.concatenate(parts, axis=0)

    def similar(unit, r, k):
        return lax.dot_general(
            unit, weights(r, k), (((1,), (1,)), ((), ())), preferred_element_type=jnp.float32
        )

    def step(g, units, rows):
        @pl.when(g + 1 < groups)
        def _():
            load_resid(g + 1).wait()

        following = []
        for p in range(GROUP):
            following.append(embed(jnp.minimum(g + 1, groups - 1) * GROUP + p, rows))
            r = g * GROUP + p
            for k in range(TILES):
                sim = similar(units[p], r, k)
                best[k, pl.ds(r, 1), :] = jnp.max(sim, axis=0, keepdims=True)
        return tuple(following)

    units = tuple(embed(p, ptok) for p in range(GROUP))
    load_members.wait()
    load_q.wait()
    begin = 0
    for c in range(ptok // TB, 0, -1):
        units = tuple(unit[: c * TB] for unit in units)
        units = lax.fori_loop(begin, ends[c - 1], lambda g, held, rows=c * TB: step(g, held, rows), units)
        begin = ends[c - 1]

    used = lax.div(order[3, 0] + wide - 1, wide)

    @pl.loop(TILES, used)
    def _(k):
        best[k] = jnp.zeros(best.shape[1:], jnp.float32)

    @pl.loop(0, order[6, 0])
    def _(m):
        r = order[5, m]

        @pl.loop(TILES, lax.div(order[2, r] + wide - 1, wide))
        def _(k):
            sim = similar(embeds[r], r, k)
            token = lax.broadcasted_iota(jnp.int32, sim.shape, 0)
            sim = jnp.where(token < order[1, r], sim, LOW)
            best[k, pl.ds(r, 1), :] = jnp.max(sim, axis=0, keepdims=True)

    from_lane = lax.div(lax.broadcasted_iota(jnp.int32, (256, queries), 0), tokens)
    to_lane = lax.broadcasted_iota(jnp.int32, (256, queries), 1)

    def gather_sum(k, total_sum):
        adder = (from_lane + k * wide == to_lane).astype(jnp.float32)
        return total_sum + jnp.dot(
            best[k], adder, precision=lax.Precision.HIGHEST, preferred_element_type=jnp.float32
        )

    sums = jnp.zeros((passages, queries), jnp.float32)
    for k in range(TILES):
        sums = gather_sum(k, sums)
    sums = lax.fori_loop(TILES, used, gather_sum, sums)
    scores[...] = jnp.take_along_axis(sums, place_ref[...], axis=1)

    cand = cand_ref[...]

    def pick(r, picked):
        return jnp.where(cand == order[0, r], scores[pl.ds(r, 1), :], picked)

    picked = lax.fori_loop(0, passages, pick, jnp.zeros((slots, queries), jnp.float32), unroll=8)
    place = lax.broadcasted_iota(jnp.int32, (slots, queries), 0)
    values = jnp.where(place < live_ref[...], picked, NEG)
    place_out = lax.broadcasted_iota(jnp.int32, (16, queries), 0)
    tops = jnp.zeros((16, queries), jnp.float32)
    for k in range(slots // 4):
        top = jnp.max(values, axis=0, keepdims=True)
        tops = jnp.where(place_out == k, top, tops)
        at = jnp.min(jnp.where(values == top, place, slots), axis=0, keepdims=True)
        values = jnp.where(place == at, LOW, values)
    padded = jnp.concatenate([tops, jnp.zeros((128 - 16, queries), jnp.float32)], axis=0)
    out_ref[...] = padded.T


def score(table, refs, order, members, place, resid, rows, cand, live):
    passages = order.shape[1]
    slots, queries = cand.shape
    ptok = resid.shape[1]
    vmem = pl.BlockSpec(memory_space=pltpu.VMEM)
    smem = pl.BlockSpec(memory_space=pltpu.SMEM)
    hbm = pl.BlockSpec(memory_space=pl.ANY)
    return pl.pallas_call(
        score_kernel,
        out_shape=jax.ShapeDtypeStruct((queries, 128), jnp.float32),
        in_specs=[smem, hbm, hbm, vmem, vmem, hbm, hbm, hbm, vmem, vmem],
        out_specs=vmem,
        scratch_shapes=[
            pltpu.SMEM((passages * ptok,), jnp.int32),
            pltpu.SMEM(members.shape, jnp.int32),
            pltpu.VMEM(table.shape, jnp.bfloat16),
            pltpu.VMEM((table.shape[0], 128), jnp.float32),
            pltpu.VMEM(resid.shape, jnp.float32),
            pltpu.VMEM(rows.shape, jnp.bfloat16),
            pltpu.VMEM(resid.shape, jnp.bfloat16),
            pltpu.VMEM((queries // 8, passages, 256), jnp.float32),
            pltpu.VMEM((passages, queries), jnp.float32),
            pltpu.SemaphoreType.DMA,
            pltpu.SemaphoreType.DMA,
            pltpu.SemaphoreType.DMA((8,)),
            pltpu.SemaphoreType.DMA((passages // GROUP,)),
            pltpu.SemaphoreType.DMA,
        ],
        compiler_params=pltpu.CompilerParams(vmem_limit_bytes=56 * 2**20),
    )(order, refs.reshape(-1), members, order, place, table, resid, rows, cand, live)


def swap_kernel(tops, inbox, outbox, mid, row_send, row_recv, send, recv):
    me, z = lax.axis_index("cent"), lax.axis_index("qry")
    wide, deep, cores = CENT_AXES
    line_size = deep * cores
    mx, mr = lax.div(me, line_size), lax.rem(me, line_size)
    per = outbox.shape[2]

    def in_row(i):
        return mx * line_size + lax.rem(mr + i, line_size)

    def in_column(i):
        return lax.rem(mx + i, wide) * line_size + mr

    barrier = pltpu.get_barrier_semaphore()
    for i in range(1, line_size):
        pl.semaphore_signal(barrier, inc=1, device_id=(in_row(i), z), device_id_type=MESH)
    for i in range(1, wide):
        pl.semaphore_signal(barrier, inc=1, device_id=(in_column(i), z), device_id_type=MESH)
    for x in range(wide):
        for r in range(line_size):
            at = (x * line_size + r) * per
            outbox[r, x] = tops[at : at + per, :]
    mid[mr] = outbox[mr]
    pl.semaphore_wait(barrier, line_size + wide - 2)

    def remote(src, dst, send_sem, recv_sem, peer):
        return pltpu.make_async_remote_copy(
            src_ref=src, dst_ref=dst, send_sem=send_sem, recv_sem=recv_sem, device_id=(peer, z), device_id_type=MESH
        )

    for i in range(1, line_size):
        remote(outbox.at[lax.rem(mr + i, line_size)], mid.at[mr], row_send, row_recv, in_row(i)).start()
    most = pl.ds(0, line_size - 1)
    remote(outbox.at[most], mid.at[most], row_send, row_recv, in_row(1)).wait()
    for i in range(1, wide):
        remote(mid.at[:, lax.rem(mx + i, wide)], inbox.at[mx], send, recv, in_column(i)).start()
    inbox[mx] = mid[:, mx]
    most = pl.ds(0, wide - 1)
    remote(inbox.at[most], inbox.at[most], send, recv, in_column(1)).wait()


def swap(tops, per):
    n = lax.axis_size("cent")
    wide, deep, cores = CENT_AXES
    vmem = pl.BlockSpec(memory_space=pltpu.VMEM)
    dma = pltpu.SemaphoreType.DMA
    inbox = pl.pallas_call(
        swap_kernel,
        out_shape=jax.ShapeDtypeStruct((wide, deep * cores, per, 128), jnp.float32),
        in_specs=[vmem],
        out_specs=vmem,
        scratch_shapes=[
            pltpu.VMEM((deep * cores, wide, per, 128), jnp.float32),
            pltpu.VMEM((deep * cores, wide, per, 128), jnp.float32),
            dma, dma, dma, dma,
        ],
        compiler_params=pltpu.CompilerParams(collective_id=1, has_side_effects=True),
    )(tops)
    return inbox.reshape(n, per, 128)


def merge_kernel(inbox, shard_out, best_out):
    n, per = inbox.shape[:2]
    keep = shard_out.shape[0]
    lists = [inbox[:, q, :] for q in range(per)]
    column = jnp.concatenate(lists, axis=0)
    across = column.T
    width = per * n
    row = across[0:16, :]
    for q in range(per):
        shard_out[:, q, :] = row[:keep, q * n : (q + 1) * n]
    lane = lax.broadcasted_iota(jnp.int32, (16, width), 1)
    shard = lax.rem(lane, n)
    place = lax.broadcasted_iota(jnp.int32, (16, width), 0)

    rank = place
    for r in range(1, n):
        near = pltpu.roll(row, r, 1)
        far = pltpu.roll(row, r + width - n, 1)
        wrapped = shard < r
        other = jnp.where(wrapped, far, near)
        for k in range(keep):
            rival = other[k : k + 1, :]
            ahead = (rival > row) | ((rival == row) & ~wrapped)
            rank = rank + ahead.astype(jnp.int32)
    ranks = jnp.concatenate([rank, jnp.zeros((width - 16, width), jnp.int32)], axis=0).T
    target = lax.broadcasted_iota(jnp.int32, (width, 128), 1)
    found = jnp.zeros((width, 128), jnp.float32)
    for k in range(keep):
        found = found + jnp.where(ranks[:, k : k + 1] == target, column[:, k : k + 1], 0.0)
    for q in range(per):
        best = jnp.sum(found[q * n : (q + 1) * n, :], axis=0, keepdims=True)
        best_out[q : q + 1, :] = best[:, :TOPK]


def merge(inbox, keep):
    n, per, _ = inbox.shape
    vmem = pl.BlockSpec(memory_space=pltpu.VMEM)
    return pl.pallas_call(
        merge_kernel,
        out_shape=(
            jax.ShapeDtypeStruct((keep, per, n), jnp.float32),
            jax.ShapeDtypeStruct((per, TOPK), jnp.float32),
        ),
        in_specs=[vmem],
        out_specs=(vmem, vmem),
    )(inbox)


def local(
    queries,
    centroids,
    shard_table,
    token_refs,
    packed_residual_buckets,
    passage_lengths,
    bucket_values,
    candidates,
    live_counts,
):
    n, nz = lax.axis_size("cent"), lax.axis_size("qry")
    per, tokens, width = queries.shape[1:]
    z = lax.axis_index("qry")
    by_owner = shard_table.reshape(n, nz, -1)
    wanted = jnp.concatenate(
        [lax.dynamic_slice_in_dim(by_owner, quarter, 1, 1) for quarter in (z, lax.rem(z + 2, nz))], axis=1
    )
    wanted = jnp.swapaxes(wanted.reshape((CENT_AXES[0], n // CENT_AXES[0]) + wanted.shape[1:]), 0, 1)
    cand, live = candidates[0, 0].T, live_counts[0]
    table, resid, rows, order, members, place = fetch(
        centroids, wanted, queries.reshape(per * tokens, width), passage_lengths[None, :], packed_residual_buckets,
        bucket_values, cand, live,
    )
    tops = score(
        table.reshape(-1, width), token_refs, order, members, place, resid, rows.reshape(-1, width), cand, live
    )
    shard_tops, best_scores = merge(swap(tops, per), candidates.shape[3] // 4)
    return (jnp.transpose(shard_tops, (1, 2, 0))[None], best_scores[None])


def solution(mesh):
    return jax.shard_map(
        local,
        mesh=mesh,
        in_specs=(
            P("qry", "cent", None, None),
            P("cent", None),
            P("cent", None),
            P("cent", None),
            P("cent", None, None),
            P("cent"),
            P(),
            P("qry", "cent", None, None),
            P("qry", "cent", None),
        ),
        out_specs=(P("qry", "cent", None, None), P("qry", "cent", None)),
        check_vma=False,
    )
```

```python
import jax
import jax.numpy as jnp
from jax import lax
from jax.experimental import pallas as pl
from jax.experimental.pallas import tpu as pltpu
from jax.sharding import PartitionSpec as P

TOPK = 100
NEG = -1e30
EPS = 1e-6
LOW = float("-inf")
TB = 16
GROUP = 4
TILES = 4
MESH = pl.DeviceIdType.MESH
CENT_AXES = (4, 4, 2)
HOPS = (
    (1, 0), (0, 1), (3, 0), (0, 3), (1, 1), (3, 3), (1, 3), (3, 1),
    (2, 0), (0, 2), (2, 1), (1, 2), (2, 3), (3, 2), (2, 2),
)
PART = 128


def place_of(me):
    wide, deep, cores = CENT_AXES
    return lax.div(me, deep * cores), lax.rem(lax.div(me, cores), deep), lax.rem(me, cores)


def peer_of(me, i, sign):
    wide, deep, cores = CENT_AXES
    x, y, core = place_of(me)
    many = len(HOPS)
    j, other = lax.rem(i - 1, many), lax.div(i - 1, many)
    code = 0
    for t, (dx, dy) in enumerate(HOPS):
        code = code + jnp.where(j == t, dx * deep + dy, 0)
    last = i == cores * many + 1
    code = jnp.where(last, 0, code)
    other = jnp.where(last, 1, other)
    dx, dy = lax.div(code, deep), lax.rem(code, deep)
    if sign < 0:
        dx, dy = wide - dx, deep - dy
    x, y, core = lax.rem(x + dx, wide), lax.rem(y + dy, deep), lax.rem(core + other, cores)
    return (x * deep + y) * cores + core


def fetch_kernel(
    cent_hbm, wanted, own, lengths, packed_hbm, buckets, cand, live, tab, resid_hbm, qall, order, members, place,
    packed, stage, cent, mid, asked, asked_s, sbuf, spread, resid, spots, order_s,
    packed_sem, stage_sem, asked_sem, order_sem, own_sem, resid_sem, off_send, off_recv, row_send, row_recv,
    q_send, q_recv, q_row_send, q_row_recv, pair_send, pair_recv, blk_send, blk_recv, half_recv, z_send, left_recv, right_recv,
):
    me, z = lax.axis_index("cent"), lax.axis_index("qry")
    n, nz = lax.axis_size("cent"), lax.axis_size("qry")
    wide, deep, cores = CENT_AXES
    line_size = deep * cores
    mx, my, core = place_of(me)
    mr = lax.rem(me, line_size)
    right, far, left = lax.rem(z + 1, nz), lax.rem(z + 2, nz), lax.rem(z + 3, nz)
    rows = tab.shape[2]
    part = sbuf.shape[1] - rows
    slots, queries = cand.shape
    pieces = stage_sem.shape[0]
    depth = stage.shape[0] // pieces
    passages = packed.shape[0]
    ptok = packed.shape[2]

    loads = [
        pltpu.make_async_copy(
            cent_hbm.at[i * depth : (i + 1) * depth], stage.at[i * depth : (i + 1) * depth], stage_sem.at[i]
        )
        for i in range(pieces)
    ]
    for load in loads:
        load.start()

    load_packed = pltpu.make_async_copy(packed_hbm, packed, packed_sem)
    load_packed.start()

    def in_row(i):
        return mx * line_size + lax.rem(mr + i, line_size)

    def in_column(i):
        return lax.rem(mx + i, wide) * line_size + mr

    barrier = pltpu.get_barrier_semaphore()
    for i in range(1, line_size):
        pl.semaphore_signal(barrier, inc=1, device_id=(in_row(i), z), device_id_type=MESH)
    for i in range(1, wide):
        pl.semaphore_signal(barrier, inc=1, device_id=(in_column(i), z), device_id_type=MESH)
    for side in (left, right):
        pl.semaphore_signal(barrier, inc=1, device_id=(me, side), device_id_type=MESH)

    across = jnp.broadcast_to(lengths[...], (passages, passages))
    down = across.T
    line = lax.broadcasted_iota(jnp.int32, (passages, passages), 0)
    lane = lax.broadcasted_iota(jnp.int32, (passages, passages), 1)
    ahead = (down > across) | ((down == across) & (line < lane))
    rank = jnp.sum(ahead.astype(jnp.int32), axis=0, keepdims=True)
    hit = jnp.broadcast_to(rank, (passages, passages)).T == lane
    order[0:1, :] = jnp.sum(jnp.where(hit, line, 0), axis=0, keepdims=True)
    order[1:2, :] = jnp.sum(jnp.where(hit, down, 0), axis=0, keepdims=True)
    lens = order[1:2, :]
    owner_of = jnp.broadcast_to(order[0:1, :], (passages, queries)).T

    def mark(slot, need):
        hit = (owner_of == cand[pl.ds(slot, 1), :]) & (live[...] > slot)
        return jnp.where(hit, 1.0, need)

    need = lax.fori_loop(0, slots, mark, jnp.zeros((passages, queries), jnp.float32), unroll=4)
    flags = need.astype(jnp.bfloat16)
    before = (line < lane).astype(jnp.bfloat16)
    spot = jnp.dot(flags, before, preferred_element_type=jnp.float32)
    place[...] = jnp.where(need > 0, spot, 0.0).astype(jnp.int32)
    spots[...] = jnp.where(need > 0, spot, -1.0)
    across_lanes = (((1,), (1,)), ((), ()))
    counts = lax.dot_general(
        jnp.ones((8, queries), jnp.bfloat16), flags, across_lanes, preferred_element_type=jnp.float32
    )[0:1]
    order[2:3, :] = counts.astype(jnp.int32)
    order[3:4, :] = jnp.broadcast_to(jnp.max(counts, axis=1, keepdims=True), (1, passages)).astype(jnp.int32)
    heads = jnp.where((lane % GROUP == 0) & (lens > line * TB), 1.0, 0.0).astype(jnp.bfloat16)
    order[4:5, :] = lax.dot_general(
        jnp.ones((8, passages), jnp.bfloat16), heads, across_lanes, preferred_element_type=jnp.float32
    )[0:1].astype(jnp.int32)
    most = TILES * (256 * queries // (own.shape[0] * n))
    number = lax.broadcasted_iota(jnp.int32, (8, queries), 1).astype(jnp.float32).astype(jnp.bfloat16)
    index = lax.broadcasted_iota(jnp.int32, (queries, queries), 0).astype(jnp.float32)
    over = jnp.broadcast_to(counts, (8, passages)) > most
    over_flags = jnp.where(over, 1.0, 0.0)
    over_spot = jnp.dot(over_flags.astype(jnp.bfloat16), before, preferred_element_type=jnp.float32)
    over_hit = jnp.where(jnp.where(over, over_spot, -1.0)[0:1] == index, 1.0, 0.0).astype(jnp.bfloat16)
    order[5:6, :] = lax.dot_general(number, over_hit, across_lanes, preferred_element_type=jnp.float32)[0:1].astype(
        jnp.int32
    )
    over_count = jnp.sum(over_flags[0:1], axis=1, keepdims=True)
    order[6:7, :] = jnp.broadcast_to(over_count, (1, passages)).astype(jnp.int32)
    order[7:8, :] = jnp.zeros((1, passages), jnp.int32)
    to_order = pltpu.make_async_copy(order, order_s, order_sem)
    to_order.start()
    for b in range(4):
        spread[b] = jnp.broadcast_to(buckets[b : b + 1, :], (ptok, 128)).T

    def widen(first, last):
        for i in range(first, last):
            loads[i].wait()

            @pl.loop(0, depth // 512)
            def _(j):
                at = pl.ds(pl.multiple_of(i * depth + j * 512, 512), 512)
                cent[at, :] = stage[at, :].astype(jnp.float32)

    widen(0, pieces // 2)
    pl.semaphore_wait(barrier, line_size + wide)

    def remote(src, dst, send, recv, peer):
        return pltpu.make_async_remote_copy(
            src_ref=src, dst_ref=dst, send_sem=send, recv_sem=recv, device_id=(peer, z), device_id_type=MESH
        )

    for i in range(1, line_size):
        remote(wanted.at[:, lax.rem(mr + i, line_size)], mid.at[mr], off_send, off_recv, in_row(i)).start()
    for i in range(1, wide):
        remote(own, qall.at[mx, my, core], q_send, q_recv, in_column(i)).start()
    mid[mr] = wanted[:, mr]
    keep_queries = pltpu.make_async_copy(own, qall.at[mx, my, core], own_sem.at[2])
    keep_queries.start()
    widen(pieces // 2, pieces)
    to_order.wait()
    load_packed.wait()
    first = remote(
        mid.at[pl.ds(0, line_size - 1)], mid.at[pl.ds(0, line_size - 1)], off_send, off_recv, in_row(1)
    )
    first.wait_recv()
    for i in range(1, wide):
        remote(mid.at[:, lax.rem(mx + i, wide)], asked.at[mx], row_send, row_recv, in_column(i)).start()
    asked[mx] = mid[:, mx]
    remote(qall.at[pl.ds(0, wide - 1), 0, 0], qall.at[pl.ds(0, wide - 1), 0, 0], q_send, q_recv, in_column(1)).wait_recv()
    keep_queries.wait()
    for i in range(1, deep):
        peer = (mx * deep + lax.rem(my + i, deep)) * cores + core
        remote(qall.at[:, my, core], qall.at[:, my, core], q_row_send, q_row_recv, peer).start()
    second = remote(
        asked.at[pl.ds(0, wide - 1)], asked.at[pl.ds(0, wide - 1)], row_send, row_recv, in_column(1)
    )
    second.wait_recv()
    to_scalar = [
        pltpu.make_async_copy(asked.at[:, :, quarter], asked_s.at[:, :, line_at], asked_sem.at[line_at])
        for line_at, quarter in enumerate((z, far))
    ]
    for copy in to_scalar:
        copy.start()
    for copy in to_scalar:
        copy.wait()

    sub = lax.broadcasted_iota(jnp.int32, (16, 128), 0)

    def pull(i, peer, line, start, count):
        px, pr = lax.div(peer, line_size), lax.rem(peer, line_size)
        for r in range(0, count, 16):
            tile = jnp.broadcast_to(cent[pl.ds(asked_s[px, pr, line, r], 1), :], (16, 128))
            for k in range(1, 16):
                value = jnp.broadcast_to(cent[pl.ds(asked_s[px, pr, line, r + k], 1), :], (16, 128))
                tile = jnp.where(sub == k, value, tile)
            sbuf[i, start + r : start + r + 16, :] = tile.astype(jnp.bfloat16)

    def block_copy(i, peer):
        return remote(sbuf.at[i, pl.ds(0, rows)], tab.at[me, z], blk_send, blk_recv.at[i], peer)

    pull(0, me, 0, 0, rows)
    keep_own = pltpu.make_async_copy(sbuf.at[0, pl.ds(0, rows)], tab.at[me, z], own_sem.at[0])
    keep_own.start()

    @pl.loop(1, n)
    def _(i):
        peer = peer_of(me, i, 1)
        pull(i, peer, 0, 0, rows)
        block_copy(i, peer).start()

    def along(ref, side, recv):
        return pltpu.make_async_remote_copy(
            src_ref=ref, dst_ref=ref, send_sem=z_send, recv_sem=recv, device_id=(me, side), device_id_type=MESH,
        )

    def forward(owner):
        along(tab.at[owner, z], right, left_recv).start()
        along(tab.at[owner, z], left, right_recv).start()

    def decode(i):
        words = packed[order_s[0, i]]
        digits = jnp.concatenate([(words >> (2 * k)) & 3 for k in range(8)], axis=0)
        low = jnp.where(digits == 0, spread[0], spread[1])
        high = jnp.where(digits == 2, spread[2], spread[3])
        value = jnp.where(digits < 2, low, high)
        resid[i] = value.T

    def enlist(i):
        hit = jnp.where(spots[pl.ds(i, 1), :] == index, 1.0, 0.0).astype(jnp.bfloat16)
        listed = lax.dot_general(number, hit, across_lanes, preferred_element_type=jnp.float32)
        members[pl.ds(i, 1), :] = listed[0:1].astype(jnp.int32)

    def extras(k, peer):
        for j in range(passages // n):
            decode(k * (passages // n) + j)
            enlist(k * (passages // n) + j)
        pull(k, peer, 1, rows, part)

    def save(g):
        at = pl.ds(g * 8, 8)
        return pltpu.make_async_copy(resid.at[at], resid_hbm.at[at], resid_sem)

    def bulk(ref, send, recv):
        return pltpu.make_async_remote_copy(
            src_ref=ref, dst_ref=ref, send_sem=send, recv_sem=recv, device_id=(me, right), device_id_type=MESH,
        )

    keep_own.wait()
    forward(me)
    extras(0, me)
    keep_half = pltpu.make_async_copy(sbuf.at[0, pl.ds(rows, part)], tab.at[me, far, pl.ds(0, part)], own_sem.at[1])
    keep_half.start()

    def relay(k):
        peer = peer_of(me, k, 1)
        block_copy(k, peer).wait_recv()
        forward(peer_of(me, k, -1))
        extras(k, peer)
        remote(
            sbuf.at[k, pl.ds(rows, part)], tab.at[me, far, pl.ds(0, part)], blk_send, half_recv, peer
        ).start()

        @pl.when(lax.rem(k, 2) == 1)
        def _():
            save(lax.div(k, 2)).start()

    @pl.loop(1, n // 2)
    def _(k):
        relay(k)

    bulk(qall.at[pl.ds(0, wide), pl.ds(0, deep - 1), 0], q_row_send, q_row_recv).wait_recv()
    pair = remote(qall.at[:, :, core], qall.at[:, :, core], pair_send, pair_recv, me + 1 - 2 * core)
    pair.start()

    @pl.loop(n // 2, n)
    def _(k):
        relay(k)

    pair.wait()
    bulk(tab.at[pl.ds(0, n // nz)], z_send, left_recv).wait_recv()
    bulk(tab.at[pl.ds(0, n // nz)], z_send, right_recv).wait_recv()
    bulk(sbuf.at[pl.ds(0, n - 1), pl.ds(rows, part)], z_send, half_recv).wait_recv()
    keep_half.wait()
    pltpu.make_async_copy(resid, resid_hbm, resid_sem).wait()
    first.wait_send()
    second.wait_send()
    bulk(qall.at[pl.ds(0, wide - 1), 0, 0], q_send, q_recv).wait_send()
    bulk(qall.at[pl.ds(0, wide), pl.ds(0, deep - 1), 0], q_row_send, q_row_recv).wait_send()
    bulk(sbuf.at[pl.ds(0, n - 1)], blk_send, q_recv).wait_send()
    bulk(tab.at[pl.ds(0, 2 * n // nz)], z_send, q_recv).wait_send()


def fetch(centroids, wanted, own, lengths, packed, buckets, cand, live):
    n, nz = lax.axis_size("cent"), lax.axis_size("qry")
    wide, deep, cores = CENT_AXES
    rows = wanted.shape[3]
    part = PART
    passages, _, ptok = packed.shape
    vmem = pl.BlockSpec(memory_space=pltpu.VMEM)
    hbm = pl.BlockSpec(memory_space=pl.ANY)
    dma = pltpu.SemaphoreType.DMA
    queries = cand.shape[1]
    return pl.pallas_call(
        fetch_kernel,
        out_shape=(
            jax.ShapeDtypeStruct((n, nz, rows, 128), jnp.bfloat16),
            jax.ShapeDtypeStruct((passages, ptok, 128), jnp.float32),
            jax.ShapeDtypeStruct(CENT_AXES + own.shape, jnp.bfloat16),
            jax.ShapeDtypeStruct((8, passages), jnp.int32),
            jax.ShapeDtypeStruct((passages, queries), jnp.int32),
            jax.ShapeDtypeStruct((passages, queries), jnp.int32),
        ),
        in_specs=[hbm, vmem, vmem, vmem, hbm, vmem, vmem, vmem],
        out_specs=(hbm, hbm, hbm, vmem, vmem, vmem),
        scratch_shapes=[
            pltpu.VMEM(packed.shape, jnp.int32),
            pltpu.VMEM(centroids.shape, jnp.bfloat16),
            pltpu.VMEM(centroids.shape, jnp.float32),
            pltpu.VMEM((deep * cores, wide, nz, rows), jnp.int32),
            pltpu.VMEM((wide, deep * cores, nz, rows), jnp.int32),
            pltpu.SMEM((wide, deep * cores, 2, rows), jnp.int32),
            pltpu.VMEM((n, rows + part, 128), jnp.bfloat16),
            pltpu.VMEM((4, 128, ptok), jnp.float32),
            pltpu.VMEM((passages, ptok, 128), jnp.float32),
            pltpu.VMEM((passages, queries), jnp.float32),
            pltpu.SMEM((8, passages), jnp.int32),
            dma, dma((8,)), dma((2,)), dma, dma((3,)), dma, dma, dma, dma, dma,
            dma, dma, dma, dma, dma, dma, dma, dma((n,)), dma, dma, dma, dma,
        ],
        compiler_params=pltpu.CompilerParams(
            collective_id=0, has_side_effects=True, vmem_limit_bytes=58 * 2**20
        ),
    )(centroids, wanted, own, lengths, packed, buckets, cand, live)


def score_kernel(
    order, refs_hbm, members_hbm, order_ref, place_ref, table_hbm, resid_hbm, q_hbm, cand_ref, live_ref,
    out_ref, refs, members, stage, tab, resid, q_ref, embeds, best, scores, refs_sem, members_sem, stage_sem, resid_sem, q_sem,
):
    passages = order.shape[1]
    groups = passages // GROUP
    slots, queries = cand_ref.shape
    ptok = resid_hbm.shape[1]
    tokens = q_hbm.shape[0] // queries
    wide = 256 // tokens
    pieces = stage_sem.shape[0]
    depth = stage.shape[0] // pieces
    loads = [
        pltpu.make_async_copy(
            table_hbm.at[i * depth : (i + 1) * depth], stage.at[i * depth : (i + 1) * depth], stage_sem.at[i]
        )
        for i in range(pieces)
    ]
    load_refs = pltpu.make_async_copy(refs_hbm, refs, refs_sem)
    load_refs.start()
    for load in loads:
        load.start()

    def load_resid(g):
        at = pl.ds(g * GROUP, GROUP)
        return pltpu.make_async_copy(resid_hbm.at[at], resid.at[at], resid_sem.at[g])

    load_members = pltpu.make_async_copy(members_hbm, members, members_sem)
    load_q = pltpu.make_async_copy(q_hbm, q_ref, q_sem)
    load_resid(0).start()

    ends = [order[4, c] for c in range(ptok // TB)]

    for i, load in enumerate(loads):
        load.wait()
        if i == pieces - 2:
            load_members.start()
            load_q.start()

            @pl.loop(1, groups)
            def _(g):
                load_resid(g).start()

        @pl.loop(0, depth // 512)
        def _(j):
            at = pl.ds(pl.multiple_of(i * depth + j * 512, 512), 512)
            tab[at, :] = stage[at, :].astype(jnp.float32)

    load_refs.wait()
    load_resid(0).wait()
    sub = lax.broadcasted_iota(jnp.int32, (8, 128), 0)

    def embed(r, rows):
        source = order[0, r] * ptok
        tiles = []
        for t in range(0, rows, 8):
            tile = jnp.broadcast_to(tab[pl.ds(refs[source + t], 1), :], (8, 128))
            for p in range(1, 8):
                row = jnp.broadcast_to(tab[pl.ds(refs[source + t + p], 1), :], (8, 128))
                tile = jnp.where(sub == p, row, tile)
            tiles.append(tile)
        summed = jnp.concatenate(tiles, axis=0) + resid[r, 0:rows, :]
        norm = jnp.sum(summed * summed, axis=1, keepdims=True)
        unit = summed * lax.rsqrt(norm + EPS)
        line = lax.broadcasted_iota(jnp.int32, unit.shape, 0)
        unit = jnp.where(line < order[1, r], unit, unit[0:1]).astype(jnp.bfloat16)
        embeds[r, 0:rows, :] = unit
        return unit

    def weights(r, k):
        parts = []
        for j in range(wide):
            at = pl.multiple_of(members[r, k * wide + j] * tokens, tokens)
            parts.append(q_ref[pl.ds(at, tokens), :])
        return jnp.concatenate(parts, axis=0)

    def similar(unit, r, k):
        return lax.dot_general(
            unit, weights(r, k), (((1,), (1,)), ((), ())), preferred_element_type=jnp.float32
        )

    def step(g, units, rows):
        @pl.when(g + 1 < groups)
        def _():
            load_resid(g + 1).wait()

        following = []
        for p in range(GROUP):
            following.append(embed(jnp.minimum(g + 1, groups - 1) * GROUP + p, rows))
            r = g * GROUP + p
            for k in range(TILES):
                sim = similar(units[p], r, k)
                best[k, pl.ds(r, 1), :] = jnp.max(sim, axis=0, keepdims=True)
        return tuple(following)

    units = tuple(embed(p, ptok) for p in range(GROUP))
    load_members.wait()
    load_q.wait()
    begin = 0
    for c in range(ptok // TB, 0, -1):
        units = tuple(unit[: c * TB] for unit in units)
        units = lax.fori_loop(begin, ends[c - 1], lambda g, held, rows=c * TB: step(g, held, rows), units)
        begin = ends[c - 1]

    used = lax.div(order[3, 0] + wide - 1, wide)

    @pl.loop(TILES, used)
    def _(k):
        best[k] = jnp.zeros(best.shape[1:], jnp.float32)

    @pl.loop(0, order[6, 0])
    def _(m):
        r = order[5, m]

        @pl.loop(TILES, lax.div(order[2, r] + wide - 1, wide))
        def _(k):
            sim = similar(embeds[r], r, k)
            token = lax.broadcasted_iota(jnp.int32, sim.shape, 0)
            sim = jnp.where(token < order[1, r], sim, LOW)
            best[k, pl.ds(r, 1), :] = jnp.max(sim, axis=0, keepdims=True)

    from_lane = lax.div(lax.broadcasted_iota(jnp.int32, (256, queries), 0), tokens)
    to_lane = lax.broadcasted_iota(jnp.int32, (256, queries), 1)

    def gather_sum(k, total_sum):
        adder = (from_lane + k * wide == to_lane).astype(jnp.float32)
        return total_sum + jnp.dot(
            best[k], adder, precision=lax.Precision.HIGHEST, preferred_element_type=jnp.float32
        )

    sums = jnp.zeros((passages, queries), jnp.float32)
    for k in range(TILES):
        sums = gather_sum(k, sums)
    sums = lax.fori_loop(TILES, used, gather_sum, sums)
    scores[...] = jnp.take_along_axis(sums, place_ref[...], axis=1)

    cand = cand_ref[...]

    def pick(r, picked):
        return jnp.where(cand == order[0, r], scores[pl.ds(r, 1), :], picked)

    picked = lax.fori_loop(0, passages, pick, jnp.zeros((slots, queries), jnp.float32), unroll=8)
    place = lax.broadcasted_iota(jnp.int32, (slots, queries), 0)
    values = jnp.where(place < live_ref[...], picked, NEG)
    place_out = lax.broadcasted_iota(jnp.int32, (16, queries), 0)
    tops = jnp.zeros((16, queries), jnp.float32)
    for k in range(slots // 4):
        top = jnp.max(values, axis=0, keepdims=True)
        tops = jnp.where(place_out == k, top, tops)
        at = jnp.min(jnp.where(values == top, place, slots), axis=0, keepdims=True)
        values = jnp.where(place == at, LOW, values)
    padded = jnp.concatenate([tops, jnp.zeros((128 - 16, queries), jnp.float32)], axis=0)
    out_ref[...] = padded.T


def score(table, refs, order, members, place, resid, rows, cand, live):
    passages = order.shape[1]
    slots, queries = cand.shape
    ptok = resid.shape[1]
    vmem = pl.BlockSpec(memory_space=pltpu.VMEM)
    smem = pl.BlockSpec(memory_space=pltpu.SMEM)
    hbm = pl.BlockSpec(memory_space=pl.ANY)
    return pl.pallas_call(
        score_kernel,
        out_shape=jax.ShapeDtypeStruct((queries, 128), jnp.float32),
        in_specs=[smem, hbm, hbm, vmem, vmem, hbm, hbm, hbm, vmem, vmem],
        out_specs=vmem,
        scratch_shapes=[
            pltpu.SMEM((passages * ptok,), jnp.int32),
            pltpu.SMEM(members.shape, jnp.int32),
            pltpu.VMEM(table.shape, jnp.bfloat16),
            pltpu.VMEM((table.shape[0], 128), jnp.float32),
            pltpu.VMEM(resid.shape, jnp.float32),
            pltpu.VMEM(rows.shape, jnp.bfloat16),
            pltpu.VMEM(resid.shape, jnp.bfloat16),
            pltpu.VMEM((queries // 8, passages, 256), jnp.float32),
            pltpu.VMEM((passages, queries), jnp.float32),
            pltpu.SemaphoreType.DMA,
            pltpu.SemaphoreType.DMA,
            pltpu.SemaphoreType.DMA((8,)),
            pltpu.SemaphoreType.DMA((passages // GROUP,)),
            pltpu.SemaphoreType.DMA,
        ],
        compiler_params=pltpu.CompilerParams(vmem_limit_bytes=56 * 2**20),
    )(order, refs.reshape(-1), members, order, place, table, resid, rows, cand, live)


def swap_kernel(tops_hbm, inbox, tops, outbox, mid, tops_sem, row_send, row_recv, send, recv):
    me, z = lax.axis_index("cent"), lax.axis_index("qry")
    wide, deep, cores = CENT_AXES
    line_size = deep * cores
    mx, mr = lax.div(me, line_size), lax.rem(me, line_size)
    per = outbox.shape[2]

    def in_row(i):
        return mx * line_size + lax.rem(mr + i, line_size)

    def in_column(i):
        return lax.rem(mx + i, wide) * line_size + mr

    load = pltpu.make_async_copy(tops_hbm, tops, tops_sem)
    load.start()
    barrier = pltpu.get_barrier_semaphore()
    for i in range(1, line_size):
        pl.semaphore_signal(barrier, inc=1, device_id=(in_row(i), z), device_id_type=MESH)
    for i in range(1, wide):
        pl.semaphore_signal(barrier, inc=1, device_id=(in_column(i), z), device_id_type=MESH)
    load.wait()
    for x in range(wide):
        for r in range(line_size):
            at = (x * line_size + r) * per
            outbox[r, x] = tops[at : at + per, :]
    mid[mr] = outbox[mr]
    pl.semaphore_wait(barrier, line_size + wide - 2)

    def remote(src, dst, send_sem, recv_sem, peer):
        return pltpu.make_async_remote_copy(
            src_ref=src, dst_ref=dst, send_sem=send_sem, recv_sem=recv_sem, device_id=(peer, z), device_id_type=MESH
        )

    for i in range(1, line_size):
        remote(outbox.at[lax.rem(mr + i, line_size)], mid.at[mr], row_send, row_recv, in_row(i)).start()
    most = pl.ds(0, line_size - 1)
    remote(outbox.at[most], mid.at[most], row_send, row_recv, in_row(1)).wait()
    for i in range(1, wide):
        remote(mid.at[:, lax.rem(mx + i, wide)], inbox.at[mx], send, recv, in_column(i)).start()
    inbox[mx] = mid[:, mx]
    most = pl.ds(0, wide - 1)
    remote(inbox.at[most], inbox.at[most], send, recv, in_column(1)).wait()


def swap(tops, per):
    n = lax.axis_size("cent")
    wide, deep, cores = CENT_AXES
    vmem = pl.BlockSpec(memory_space=pltpu.VMEM)
    hbm = pl.BlockSpec(memory_space=pl.ANY)
    dma = pltpu.SemaphoreType.DMA
    inbox = pl.pallas_call(
        swap_kernel,
        out_shape=jax.ShapeDtypeStruct((wide, deep * cores, per, 128), jnp.float32),
        in_specs=[hbm],
        out_specs=vmem,
        scratch_shapes=[
            pltpu.VMEM(tops.shape, jnp.float32),
            pltpu.VMEM((deep * cores, wide, per, 128), jnp.float32),
            pltpu.VMEM((deep * cores, wide, per, 128), jnp.float32),
            dma, dma, dma, dma, dma,
        ],
        compiler_params=pltpu.CompilerParams(collective_id=1, has_side_effects=True),
    )(tops)
    return inbox.reshape(n, per, 128)


def merge_kernel(inbox, shard_out, best_out):
    n, per = inbox.shape[:2]
    keep = shard_out.shape[0]
    lists = [inbox[:, q, :] for q in range(per)]
    column = jnp.concatenate(lists, axis=0)
    across = column.T
    width = per * n
    row = across[0:16, :]
    for q in range(per):
        shard_out[:, q, :] = row[:keep, q * n : (q + 1) * n]
    lane = lax.broadcasted_iota(jnp.int32, (16, width), 1)
    shard = lax.rem(lane, n)
    place = lax.broadcasted_iota(jnp.int32, (16, width), 0)

    rank = place
    for r in range(1, n):
        near = pltpu.roll(row, r, 1)
        far = pltpu.roll(row, r + width - n, 1)
        wrapped = shard < r
        other = jnp.where(wrapped, far, near)
        for k in range(keep):
            rival = other[k : k + 1, :]
            ahead = (rival > row) | ((rival == row) & ~wrapped)
            rank = rank + ahead.astype(jnp.int32)
    ranks = jnp.concatenate([rank, jnp.zeros((width - 16, width), jnp.int32)], axis=0).T
    target = lax.broadcasted_iota(jnp.int32, (width, 128), 1)
    found = jnp.zeros((width, 128), jnp.float32)
    for k in range(keep):
        found = found + jnp.where(ranks[:, k : k + 1] == target, column[:, k : k + 1], 0.0)
    for q in range(per):
        best = jnp.sum(found[q * n : (q + 1) * n, :], axis=0, keepdims=True)
        best_out[q : q + 1, :] = best[:, :TOPK]


def merge(inbox, keep):
    n, per, _ = inbox.shape
    vmem = pl.BlockSpec(memory_space=pltpu.VMEM)
    return pl.pallas_call(
        merge_kernel,
        out_shape=(
            jax.ShapeDtypeStruct((keep, per, n), jnp.float32),
            jax.ShapeDtypeStruct((per, TOPK), jnp.float32),
        ),
        in_specs=[vmem],
        out_specs=(vmem, vmem),
    )(inbox)


def local(
    queries,
    centroids,
    shard_table,
    token_refs,
    packed_residual_buckets,
    passage_lengths,
    bucket_values,
    candidates,
    live_counts,
):
    n, nz = lax.axis_size("cent"), lax.axis_size("qry")
    per, tokens, width = queries.shape[1:]
    wanted = shard_table.reshape(CENT_AXES[0], n // CENT_AXES[0], nz, -1)
    cand, live = candidates[0, 0].T, live_counts[0]
    table, resid, rows, order, members, place = fetch(
        centroids, wanted, queries.reshape(per * tokens, width), passage_lengths[None, :], packed_residual_buckets,
        bucket_values, cand, live,
    )
    tops = score(
        table.reshape(-1, width), token_refs, order, members, place, resid, rows.reshape(-1, width), cand, live
    )
    shard_tops, best_scores = merge(swap(tops, per), candidates.shape[3] // 4)
    return (jnp.transpose(shard_tops, (1, 2, 0))[None], best_scores[None])


def solution(mesh):
    return jax.shard_map(
        local,
        mesh=mesh,
        in_specs=(
            P("qry", "cent", None, None),
            P("cent", None),
            P("cent", None),
            P("cent", None),
            P("cent", None, None),
            P("cent"),
            P(),
            P("qry", "cent", None, None),
            P("qry", "cent", None),
        ),
        out_specs=(P("qry", "cent", None, None), P("qry", "cent", None)),
        check_vma=False,
    )
```

```python
import jax
import jax.numpy as jnp
from jax import lax
from jax.experimental import pallas as pl
from jax.experimental.pallas import tpu as pltpu
from jax.sharding import PartitionSpec as P

TOPK = 100
NEG = -1e30
EPS = 1e-6
LOW = float("-inf")
TB = 16
GROUP = 4
TILES = 4
MESH = pl.DeviceIdType.MESH
CENT_AXES = (4, 4, 2)
HOPS = (
    (1, 0), (0, 1), (3, 0), (0, 3), (1, 1), (3, 3), (1, 3), (3, 1),
    (2, 0), (0, 2), (2, 1), (1, 2), (2, 3), (3, 2), (2, 2),
)
PART = 128


def place_of(me):
    wide, deep, cores = CENT_AXES
    return lax.div(me, deep * cores), lax.rem(lax.div(me, cores), deep), lax.rem(me, cores)


def peer_of(me, i, sign):
    wide, deep, cores = CENT_AXES
    x, y, core = place_of(me)
    many = len(HOPS)
    j, other = lax.rem(i - 1, many), lax.div(i - 1, many)
    code = 0
    for t, (dx, dy) in enumerate(HOPS):
        code = code + jnp.where(j == t, dx * deep + dy, 0)
    last = i == cores * many + 1
    code = jnp.where(last, 0, code)
    other = jnp.where(last, 1, other)
    dx, dy = lax.div(code, deep), lax.rem(code, deep)
    if sign < 0:
        dx, dy = wide - dx, deep - dy
    x, y, core = lax.rem(x + dx, wide), lax.rem(y + dy, deep), lax.rem(core + other, cores)
    return (x * deep + y) * cores + core


def fetch_kernel(
    cent_hbm, wanted, own, lengths, packed_hbm, buckets, cand, live, tab, resid_hbm, qall, order, members, place,
    packed, stage, cent, mid, asked, asked_s, sbuf, spread, resid, spots, order_s,
    packed_sem, stage_sem, asked_sem, order_sem, own_sem, resid_sem, off_send, off_recv, row_send, row_recv,
    q_send, q_recv, q_row_send, q_row_recv, pair_send, pair_recv, blk_send, blk_recv, half_recv, z_send, left_recv, right_recv,
):
    me, z = lax.axis_index("cent"), lax.axis_index("qry")
    n, nz = lax.axis_size("cent"), lax.axis_size("qry")
    wide, deep, cores = CENT_AXES
    line_size = deep * cores
    mx, my, core = place_of(me)
    mr = lax.rem(me, line_size)
    right, far, left = lax.rem(z + 1, nz), lax.rem(z + 2, nz), lax.rem(z + 3, nz)
    rows = tab.shape[2]
    part = sbuf.shape[1] - rows
    slots, queries = cand.shape
    pieces = stage_sem.shape[0]
    depth = stage.shape[0] // pieces
    passages = packed.shape[0]
    ptok = packed.shape[2]

    loads = [
        pltpu.make_async_copy(
            cent_hbm.at[i * depth : (i + 1) * depth], stage.at[i * depth : (i + 1) * depth], stage_sem.at[i]
        )
        for i in range(pieces)
    ]
    for load in loads:
        load.start()

    load_packed = pltpu.make_async_copy(packed_hbm, packed, packed_sem)
    load_packed.start()

    def in_row(i):
        return mx * line_size + lax.rem(mr + i, line_size)

    def in_column(i):
        return lax.rem(mx + i, wide) * line_size + mr

    barrier = pltpu.get_barrier_semaphore()
    for i in range(1, line_size):
        pl.semaphore_signal(barrier, inc=1, device_id=(in_row(i), z), device_id_type=MESH)
    for i in range(1, wide):
        pl.semaphore_signal(barrier, inc=1, device_id=(in_column(i), z), device_id_type=MESH)
    for side in (left, right):
        pl.semaphore_signal(barrier, inc=1, device_id=(me, side), device_id_type=MESH)

    across = jnp.broadcast_to(lengths[...], (passages, passages))
    down = across.T
    line = lax.broadcasted_iota(jnp.int32, (passages, passages), 0)
    lane = lax.broadcasted_iota(jnp.int32, (passages, passages), 1)
    ahead = (down > across) | ((down == across) & (line < lane))
    rank = jnp.sum(ahead.astype(jnp.int32), axis=0, keepdims=True)
    hit = jnp.broadcast_to(rank, (passages, passages)).T == lane
    order[0:1, :] = jnp.sum(jnp.where(hit, line, 0), axis=0, keepdims=True)
    order[1:2, :] = jnp.sum(jnp.where(hit, down, 0), axis=0, keepdims=True)
    lens = order[1:2, :]
    owner_of = jnp.broadcast_to(order[0:1, :], (passages, queries)).T

    def mark(slot, need):
        hit = (owner_of == cand[pl.ds(slot, 1), :]) & (live[...] > slot)
        return jnp.where(hit, 1.0, need)

    need = lax.fori_loop(0, slots, mark, jnp.zeros((passages, queries), jnp.float32), unroll=4)
    flags = need.astype(jnp.bfloat16)
    before = (line < lane).astype(jnp.bfloat16)
    spot = jnp.dot(flags, before, preferred_element_type=jnp.float32)
    place[...] = jnp.where(need > 0, spot, 0.0).astype(jnp.int32)
    spots[...] = jnp.where(need > 0, spot, -1.0)
    across_lanes = (((1,), (1,)), ((), ()))
    counts = lax.dot_general(
        jnp.ones((8, queries), jnp.bfloat16), flags, across_lanes, preferred_element_type=jnp.float32
    )[0:1]
    order[2:3, :] = counts.astype(jnp.int32)
    order[3:4, :] = jnp.broadcast_to(jnp.max(counts, axis=1, keepdims=True), (1, passages)).astype(jnp.int32)
    heads = jnp.where((lane % GROUP == 0) & (lens > line * TB), 1.0, 0.0).astype(jnp.bfloat16)
    order[4:5, :] = lax.dot_general(
        jnp.ones((8, passages), jnp.bfloat16), heads, across_lanes, preferred_element_type=jnp.float32
    )[0:1].astype(jnp.int32)
    most = TILES * (256 * queries // (own.shape[0] * n))
    number = lax.broadcasted_iota(jnp.int32, (8, queries), 1).astype(jnp.float32).astype(jnp.bfloat16)
    index = lax.broadcasted_iota(jnp.int32, (queries, queries), 0).astype(jnp.float32)
    over = jnp.broadcast_to(counts, (8, passages)) > most
    over_flags = jnp.where(over, 1.0, 0.0)
    over_spot = jnp.dot(over_flags.astype(jnp.bfloat16), before, preferred_element_type=jnp.float32)
    over_hit = jnp.where(jnp.where(over, over_spot, -1.0)[0:1] == index, 1.0, 0.0).astype(jnp.bfloat16)
    order[5:6, :] = lax.dot_general(number, over_hit, across_lanes, preferred_element_type=jnp.float32)[0:1].astype(
        jnp.int32
    )
    over_count = jnp.sum(over_flags[0:1], axis=1, keepdims=True)
    order[6:7, :] = jnp.broadcast_to(over_count, (1, passages)).astype(jnp.int32)
    order[7:8, :] = jnp.zeros((1, passages), jnp.int32)
    to_order = pltpu.make_async_copy(order, order_s, order_sem)
    to_order.start()
    for b in range(4):
        spread[b] = jnp.broadcast_to(buckets[b : b + 1, :], (ptok, 128)).T

    def widen(first, last):
        for i in range(first, last):
            loads[i].wait()

            @pl.loop(0, depth // 512)
            def _(j):
                at = pl.ds(pl.multiple_of(i * depth + j * 512, 512), 512)
                cent[at, :] = stage[at, :].astype(jnp.float32)

    widen(0, pieces // 2)
    pl.semaphore_wait(barrier, line_size + wide)

    def remote(src, dst, send, recv, peer):
        return pltpu.make_async_remote_copy(
            src_ref=src, dst_ref=dst, send_sem=send, recv_sem=recv, device_id=(peer, z), device_id_type=MESH
        )

    for i in range(1, line_size):
        remote(wanted.at[:, lax.rem(mr + i, line_size)], mid.at[mr], off_send, off_recv, in_row(i)).start()
    half = own.shape[0] // 2
    upper, lower = pl.ds(0, half), pl.ds(half, half)

    def beside(i):
        return (mx * deep + lax.rem(my + i, deep)) * cores + core

    for i in range(1, wide):
        remote(own.at[upper], qall.at[mx, my, core, upper], q_send, q_recv, in_column(i)).start()
        remote(own.at[lower], qall.at[mx, my, core, lower], q_send, q_recv, beside(i)).start()
    mid[mr] = wanted[:, mr]
    keep_queries = pltpu.make_async_copy(own, qall.at[mx, my, core], own_sem.at[2])
    keep_queries.start()
    widen(pieces // 2, pieces)
    to_order.wait()
    load_packed.wait()
    first = remote(
        mid.at[pl.ds(0, line_size - 1)], mid.at[pl.ds(0, line_size - 1)], off_send, off_recv, in_row(1)
    )
    first.wait_recv()
    for i in range(1, wide):
        remote(mid.at[:, lax.rem(mx + i, wide)], asked.at[mx], row_send, row_recv, in_column(i)).start()
    asked[mx] = mid[:, mx]
    remote(qall.at[pl.ds(0, wide - 1), 0, 0], qall.at[pl.ds(0, wide - 1), 0, 0], q_send, q_recv, in_column(1)).wait_recv()
    keep_queries.wait()
    for i in range(1, deep):
        corner, side_row = qall.at[:, my, core, upper], qall.at[mx, :, core, lower]
        remote(corner, corner, q_row_send, q_row_recv, beside(i)).start()
        remote(side_row, side_row, q_row_send, q_row_recv, in_column(i)).start()
    second = remote(
        asked.at[pl.ds(0, wide - 1)], asked.at[pl.ds(0, wide - 1)], row_send, row_recv, in_column(1)
    )
    second.wait_recv()
    to_scalar = [
        pltpu.make_async_copy(asked.at[:, :, quarter], asked_s.at[:, :, line_at], asked_sem.at[line_at])
        for line_at, quarter in enumerate((z, far))
    ]
    for copy in to_scalar:
        copy.start()
    for copy in to_scalar:
        copy.wait()

    sub = lax.broadcasted_iota(jnp.int32, (16, 128), 0)

    def pull(i, peer, line, start, count):
        px, pr = lax.div(peer, line_size), lax.rem(peer, line_size)
        for r in range(0, count, 16):
            tile = jnp.broadcast_to(cent[pl.ds(asked_s[px, pr, line, r], 1), :], (16, 128))
            for k in range(1, 16):
                value = jnp.broadcast_to(cent[pl.ds(asked_s[px, pr, line, r + k], 1), :], (16, 128))
                tile = jnp.where(sub == k, value, tile)
            sbuf[i, start + r : start + r + 16, :] = tile.astype(jnp.bfloat16)

    def block_copy(i, peer):
        return remote(sbuf.at[i, pl.ds(0, rows)], tab.at[me, z], blk_send, blk_recv.at[i], peer)

    pull(0, me, 0, 0, rows)
    keep_own = pltpu.make_async_copy(sbuf.at[0, pl.ds(0, rows)], tab.at[me, z], own_sem.at[0])
    keep_own.start()

    @pl.loop(1, n)
    def _(i):
        peer = peer_of(me, i, 1)
        pull(i, peer, 0, 0, rows)
        block_copy(i, peer).start()

    def along(ref, side, recv):
        return pltpu.make_async_remote_copy(
            src_ref=ref, dst_ref=ref, send_sem=z_send, recv_sem=recv, device_id=(me, side), device_id_type=MESH,
        )

    def forward(owner):
        along(tab.at[owner, z], right, left_recv).start()
        along(tab.at[owner, z], left, right_recv).start()

    def decode(i):
        words = packed[order_s[0, i]]
        digits = jnp.concatenate([(words >> (2 * k)) & 3 for k in range(8)], axis=0)
        low = jnp.where(digits == 0, spread[0], spread[1])
        high = jnp.where(digits == 2, spread[2], spread[3])
        value = jnp.where(digits < 2, low, high)
        resid[i] = value.T

    def enlist(i):
        hit = jnp.where(spots[pl.ds(i, 1), :] == index, 1.0, 0.0).astype(jnp.bfloat16)
        listed = lax.dot_general(number, hit, across_lanes, preferred_element_type=jnp.float32)
        members[pl.ds(i, 1), :] = listed[0:1].astype(jnp.int32)

    def extras(k, peer):
        for j in range(passages // n):
            decode(k * (passages // n) + j)
            enlist(k * (passages // n) + j)
        pull(k, peer, 1, rows, part)

    def save(g):
        at = pl.ds(g * 8, 8)
        return pltpu.make_async_copy(resid.at[at], resid_hbm.at[at], resid_sem)

    def bulk(ref, send, recv):
        return pltpu.make_async_remote_copy(
            src_ref=ref, dst_ref=ref, send_sem=send, recv_sem=recv, device_id=(me, right), device_id_type=MESH,
        )

    keep_own.wait()
    forward(me)
    extras(0, me)
    keep_half = pltpu.make_async_copy(sbuf.at[0, pl.ds(rows, part)], tab.at[me, far, pl.ds(0, part)], own_sem.at[1])
    keep_half.start()

    def relay(k):
        peer = peer_of(me, k, 1)
        block_copy(k, peer).wait_recv()
        forward(peer_of(me, k, -1))
        extras(k, peer)
        remote(
            sbuf.at[k, pl.ds(rows, part)], tab.at[me, far, pl.ds(0, part)], blk_send, half_recv, peer
        ).start()

        @pl.when(lax.rem(k, 2) == 1)
        def _():
            save(lax.div(k, 2)).start()

    @pl.loop(1, n // 2)
    def _(k):
        relay(k)

    bulk(qall.at[pl.ds(0, wide), pl.ds(0, deep - 1), 0], q_row_send, q_row_recv).wait_recv()
    pair = remote(qall.at[:, :, core], qall.at[:, :, core], pair_send, pair_recv, me + 1 - 2 * core)
    pair.start()

    @pl.loop(n // 2, n)
    def _(k):
        relay(k)

    pair.wait()
    bulk(tab.at[pl.ds(0, n // nz)], z_send, left_recv).wait_recv()
    bulk(tab.at[pl.ds(0, n // nz)], z_send, right_recv).wait_recv()
    bulk(sbuf.at[pl.ds(0, n - 1), pl.ds(rows, part)], z_send, half_recv).wait_recv()
    keep_half.wait()
    pltpu.make_async_copy(resid, resid_hbm, resid_sem).wait()
    first.wait_send()
    second.wait_send()
    bulk(qall.at[pl.ds(0, wide - 1), 0, 0], q_send, q_recv).wait_send()
    bulk(qall.at[pl.ds(0, wide), pl.ds(0, deep - 1), 0], q_row_send, q_row_recv).wait_send()
    bulk(sbuf.at[pl.ds(0, n - 1)], blk_send, q_recv).wait_send()
    bulk(tab.at[pl.ds(0, 2 * n // nz)], z_send, q_recv).wait_send()


def fetch(centroids, wanted, own, lengths, packed, buckets, cand, live):
    n, nz = lax.axis_size("cent"), lax.axis_size("qry")
    wide, deep, cores = CENT_AXES
    rows = wanted.shape[3]
    part = PART
    passages, _, ptok = packed.shape
    vmem = pl.BlockSpec(memory_space=pltpu.VMEM)
    hbm = pl.BlockSpec(memory_space=pl.ANY)
    dma = pltpu.SemaphoreType.DMA
    queries = cand.shape[1]
    return pl.pallas_call(
        fetch_kernel,
        out_shape=(
            jax.ShapeDtypeStruct((n, nz, rows, 128), jnp.bfloat16),
            jax.ShapeDtypeStruct((passages, ptok, 128), jnp.float32),
            jax.ShapeDtypeStruct(CENT_AXES + own.shape, jnp.bfloat16),
            jax.ShapeDtypeStruct((8, passages), jnp.int32),
            jax.ShapeDtypeStruct((passages, queries), jnp.int32),
            jax.ShapeDtypeStruct((passages, queries), jnp.int32),
        ),
        in_specs=[hbm, vmem, vmem, vmem, hbm, vmem, vmem, vmem],
        out_specs=(hbm, hbm, hbm, vmem, vmem, vmem),
        scratch_shapes=[
            pltpu.VMEM(packed.shape, jnp.int32),
            pltpu.VMEM(centroids.shape, jnp.bfloat16),
            pltpu.VMEM(centroids.shape, jnp.float32),
            pltpu.VMEM((deep * cores, wide, nz, rows), jnp.int32),
            pltpu.VMEM((wide, deep * cores, nz, rows), jnp.int32),
            pltpu.SMEM((wide, deep * cores, 2, rows), jnp.int32),
            pltpu.VMEM((n, rows + part, 128), jnp.bfloat16),
            pltpu.VMEM((4, 128, ptok), jnp.float32),
            pltpu.VMEM((passages, ptok, 128), jnp.float32),
            pltpu.VMEM((passages, queries), jnp.float32),
            pltpu.SMEM((8, passages), jnp.int32),
            dma, dma((8,)), dma((2,)), dma, dma((3,)), dma, dma, dma, dma, dma,
            dma, dma, dma, dma, dma, dma, dma, dma((n,)), dma, dma, dma, dma,
        ],
        compiler_params=pltpu.CompilerParams(
            collective_id=0, has_side_effects=True, vmem_limit_bytes=58 * 2**20
        ),
    )(centroids, wanted, own, lengths, packed, buckets, cand, live)


def score_kernel(
    order, refs_hbm, members_hbm, order_ref, place_ref, table_hbm, resid_hbm, q_hbm, cand_ref, live_ref,
    out_ref, refs, members, stage, tab, resid, q_ref, embeds, best, scores, refs_sem, members_sem, stage_sem, resid_sem, q_sem,
):
    passages = order.shape[1]
    groups = passages // GROUP
    slots, queries = cand_ref.shape
    ptok = resid_hbm.shape[1]
    tokens = q_hbm.shape[0] // queries
    wide = 256 // tokens
    pieces = stage_sem.shape[0]
    depth = stage.shape[0] // pieces
    loads = [
        pltpu.make_async_copy(
            table_hbm.at[i * depth : (i + 1) * depth], stage.at[i * depth : (i + 1) * depth], stage_sem.at[i]
        )
        for i in range(pieces)
    ]
    load_refs = pltpu.make_async_copy(refs_hbm, refs, refs_sem)
    load_refs.start()
    for load in loads:
        load.start()

    def load_resid(g):
        at = pl.ds(g * GROUP, GROUP)
        return pltpu.make_async_copy(resid_hbm.at[at], resid.at[at], resid_sem.at[g])

    load_members = pltpu.make_async_copy(members_hbm, members, members_sem)
    load_q = pltpu.make_async_copy(q_hbm, q_ref, q_sem)
    load_resid(0).start()

    ends = [order[4, c] for c in range(ptok // TB)]

    for i, load in enumerate(loads):
        load.wait()
        if i == pieces - 2:
            load_members.start()
            load_q.start()

            @pl.loop(1, groups)
            def _(g):
                load_resid(g).start()

        @pl.loop(0, depth // 512)
        def _(j):
            at = pl.ds(pl.multiple_of(i * depth + j * 512, 512), 512)
            tab[at, :] = stage[at, :].astype(jnp.float32)

    load_refs.wait()
    load_resid(0).wait()
    sub = lax.broadcasted_iota(jnp.int32, (8, 128), 0)

    def embed(r, rows):
        source = order[0, r] * ptok
        tiles = []
        for t in range(0, rows, 8):
            tile = jnp.broadcast_to(tab[pl.ds(refs[source + t], 1), :], (8, 128))
            for p in range(1, 8):
                row = jnp.broadcast_to(tab[pl.ds(refs[source + t + p], 1), :], (8, 128))
                tile = jnp.where(sub == p, row, tile)
            tiles.append(tile)
        summed = jnp.concatenate(tiles, axis=0) + resid[r, 0:rows, :]
        norm = jnp.sum(summed * summed, axis=1, keepdims=True)
        unit = summed * lax.rsqrt(norm + EPS)
        line = lax.broadcasted_iota(jnp.int32, unit.shape, 0)
        unit = jnp.where(line < order[1, r], unit, unit[0:1]).astype(jnp.bfloat16)
        embeds[r, 0:rows, :] = unit
        return unit

    def weights(r, k):
        parts = []
        for j in range(wide):
            at = pl.multiple_of(members[r, k * wide + j] * tokens, tokens)
            parts.append(q_ref[pl.ds(at, tokens), :])
        return jnp.concatenate(parts, axis=0)

    def similar(unit, r, k):
        return lax.dot_general(
            unit, weights(r, k), (((1,), (1,)), ((), ())), preferred_element_type=jnp.float32
        )

    def step(g, units, rows):
        @pl.when(g + 1 < groups)
        def _():
            load_resid(g + 1).wait()

        following = []
        for p in range(GROUP):
            following.append(embed(jnp.minimum(g + 1, groups - 1) * GROUP + p, rows))
            r = g * GROUP + p
            for k in range(TILES):
                sim = similar(units[p], r, k)
                best[k, pl.ds(r, 1), :] = jnp.max(sim, axis=0, keepdims=True)
        return tuple(following)

    units = tuple(embed(p, ptok) for p in range(GROUP))
    load_members.wait()
    load_q.wait()
    begin = 0
    for c in range(ptok // TB, 0, -1):
        units = tuple(unit[: c * TB] for unit in units)
        units = lax.fori_loop(begin, ends[c - 1], lambda g, held, rows=c * TB: step(g, held, rows), units)
        begin = ends[c - 1]

    used = lax.div(order[3, 0] + wide - 1, wide)

    @pl.loop(TILES, used)
    def _(k):
        best[k] = jnp.zeros(best.shape[1:], jnp.float32)

    @pl.loop(0, order[6, 0])
    def _(m):
        r = order[5, m]

        @pl.loop(TILES, lax.div(order[2, r] + wide - 1, wide))
        def _(k):
            sim = similar(embeds[r], r, k)
            token = lax.broadcasted_iota(jnp.int32, sim.shape, 0)
            sim = jnp.where(token < order[1, r], sim, LOW)
            best[k, pl.ds(r, 1), :] = jnp.max(sim, axis=0, keepdims=True)

    from_lane = lax.div(lax.broadcasted_iota(jnp.int32, (256, queries), 0), tokens)
    to_lane = lax.broadcasted_iota(jnp.int32, (256, queries), 1)

    def gather_sum(k, total_sum):
        adder = (from_lane + k * wide == to_lane).astype(jnp.float32)
        return total_sum + jnp.dot(
            best[k], adder, precision=lax.Precision.HIGHEST, preferred_element_type=jnp.float32
        )

    sums = jnp.zeros((passages, queries), jnp.float32)
    for k in range(TILES):
        sums = gather_sum(k, sums)
    sums = lax.fori_loop(TILES, used, gather_sum, sums)
    scores[...] = jnp.take_along_axis(sums, place_ref[...], axis=1)

    cand = cand_ref[...]

    def pick(r, picked):
        return jnp.where(cand == order[0, r], scores[pl.ds(r, 1), :], picked)

    picked = lax.fori_loop(0, passages, pick, jnp.zeros((slots, queries), jnp.float32), unroll=8)
    place = lax.broadcasted_iota(jnp.int32, (slots, queries), 0)
    values = jnp.where(place < live_ref[...], picked, NEG)
    place_out = lax.broadcasted_iota(jnp.int32, (16, queries), 0)
    tops = jnp.zeros((16, queries), jnp.float32)
    for k in range(slots // 4):
        top = jnp.max(values, axis=0, keepdims=True)
        tops = jnp.where(place_out == k, top, tops)
        at = jnp.min(jnp.where(values == top, place, slots), axis=0, keepdims=True)
        values = jnp.where(place == at, LOW, values)
    padded = jnp.concatenate([tops, jnp.zeros((128 - 16, queries), jnp.float32)], axis=0)
    out_ref[...] = padded.T


def score(table, refs, order, members, place, resid, rows, cand, live):
    passages = order.shape[1]
    slots, queries = cand.shape
    ptok = resid.shape[1]
    vmem = pl.BlockSpec(memory_space=pltpu.VMEM)
    smem = pl.BlockSpec(memory_space=pltpu.SMEM)
    hbm = pl.BlockSpec(memory_space=pl.ANY)
    return pl.pallas_call(
        score_kernel,
        out_shape=jax.ShapeDtypeStruct((queries, 128), jnp.float32),
        in_specs=[smem, hbm, hbm, vmem, vmem, hbm, hbm, hbm, vmem, vmem],
        out_specs=vmem,
        scratch_shapes=[
            pltpu.SMEM((passages * ptok,), jnp.int32),
            pltpu.SMEM(members.shape, jnp.int32),
            pltpu.VMEM(table.shape, jnp.bfloat16),
            pltpu.VMEM((table.shape[0], 128), jnp.float32),
            pltpu.VMEM(resid.shape, jnp.float32),
            pltpu.VMEM(rows.shape, jnp.bfloat16),
            pltpu.VMEM(resid.shape, jnp.bfloat16),
            pltpu.VMEM((queries // 8, passages, 256), jnp.float32),
            pltpu.VMEM((passages, queries), jnp.float32),
            pltpu.SemaphoreType.DMA,
            pltpu.SemaphoreType.DMA,
            pltpu.SemaphoreType.DMA((8,)),
            pltpu.SemaphoreType.DMA((passages // GROUP,)),
            pltpu.SemaphoreType.DMA,
        ],
        compiler_params=pltpu.CompilerParams(vmem_limit_bytes=56 * 2**20),
    )(order, refs.reshape(-1), members, order, place, table, resid, rows, cand, live)


def swap_kernel(tops_hbm, inbox, tops, outbox, mid, tops_sem, row_send, row_recv, send, recv):
    me, z = lax.axis_index("cent"), lax.axis_index("qry")
    wide, deep, cores = CENT_AXES
    line_size = deep * cores
    mx, mr = lax.div(me, line_size), lax.rem(me, line_size)
    per = outbox.shape[2]

    def in_row(i):
        return mx * line_size + lax.rem(mr + i, line_size)

    def in_column(i):
        return lax.rem(mx + i, wide) * line_size + mr

    load = pltpu.make_async_copy(tops_hbm, tops, tops_sem)
    load.start()
    barrier = pltpu.get_barrier_semaphore()
    for i in range(1, line_size):
        pl.semaphore_signal(barrier, inc=1, device_id=(in_row(i), z), device_id_type=MESH)
    for i in range(1, wide):
        pl.semaphore_signal(barrier, inc=1, device_id=(in_column(i), z), device_id_type=MESH)
    load.wait()
    for x in range(wide):
        for r in range(line_size):
            at = (x * line_size + r) * per
            outbox[r, x] = tops[at : at + per, :]
    mid[mr] = outbox[mr]
    pl.semaphore_wait(barrier, line_size + wide - 2)

    def remote(src, dst, send_sem, recv_sem, peer):
        return pltpu.make_async_remote_copy(
            src_ref=src, dst_ref=dst, send_sem=send_sem, recv_sem=recv_sem, device_id=(peer, z), device_id_type=MESH
        )

    for i in range(1, line_size):
        remote(outbox.at[lax.rem(mr + i, line_size)], mid.at[mr], row_send, row_recv, in_row(i)).start()
    most = pl.ds(0, line_size - 1)
    remote(outbox.at[most], mid.at[most], row_send, row_recv, in_row(1)).wait()
    for i in range(1, wide):
        remote(mid.at[:, lax.rem(mx + i, wide)], inbox.at[mx], send, recv, in_column(i)).start()
    inbox[mx] = mid[:, mx]
    most = pl.ds(0, wide - 1)
    remote(inbox.at[most], inbox.at[most], send, recv, in_column(1)).wait()


def swap(tops, per):
    n = lax.axis_size("cent")
    wide, deep, cores = CENT_AXES
    vmem = pl.BlockSpec(memory_space=pltpu.VMEM)
    hbm = pl.BlockSpec(memory_space=pl.ANY)
    dma = pltpu.SemaphoreType.DMA
    inbox = pl.pallas_call(
        swap_kernel,
        out_shape=jax.ShapeDtypeStruct((wide, deep * cores, per, 128), jnp.float32),
        in_specs=[hbm],
        out_specs=vmem,
        scratch_shapes=[
            pltpu.VMEM(tops.shape, jnp.float32),
            pltpu.VMEM((deep * cores, wide, per, 128), jnp.float32),
            pltpu.VMEM((deep * cores, wide, per, 128), jnp.float32),
            dma, dma, dma, dma, dma,
        ],
        compiler_params=pltpu.CompilerParams(collective_id=1, has_side_effects=True),
    )(tops)
    return inbox.reshape(n, per, 128)


def merge_kernel(inbox, shard_out, best_out):
    n, per = inbox.shape[:2]
    keep = shard_out.shape[0]
    lists = [inbox[:, q, :] for q in range(per)]
    column = jnp.concatenate(lists, axis=0)
    across = column.T
    width = per * n
    row = across[0:16, :]
    for q in range(per):
        shard_out[:, q, :] = row[:keep, q * n : (q + 1) * n]
    lane = lax.broadcasted_iota(jnp.int32, (16, width), 1)
    shard = lax.rem(lane, n)
    place = lax.broadcasted_iota(jnp.int32, (16, width), 0)

    rank = place
    for r in range(1, n):
        near = pltpu.roll(row, r, 1)
        far = pltpu.roll(row, r + width - n, 1)
        wrapped = shard < r
        other = jnp.where(wrapped, far, near)
        for k in range(keep):
            rival = other[k : k + 1, :]
            ahead = (rival > row) | ((rival == row) & ~wrapped)
            rank = rank + ahead.astype(jnp.int32)
    ranks = jnp.concatenate([rank, jnp.zeros((width - 16, width), jnp.int32)], axis=0).T
    target = lax.broadcasted_iota(jnp.int32, (width, 128), 1)
    found = jnp.zeros((width, 128), jnp.float32)
    for k in range(keep):
        found = found + jnp.where(ranks[:, k : k + 1] == target, column[:, k : k + 1], 0.0)
    for q in range(per):
        best = jnp.sum(found[q * n : (q + 1) * n, :], axis=0, keepdims=True)
        best_out[q : q + 1, :] = best[:, :TOPK]


def merge(inbox, keep):
    n, per, _ = inbox.shape
    vmem = pl.BlockSpec(memory_space=pltpu.VMEM)
    return pl.pallas_call(
        merge_kernel,
        out_shape=(
            jax.ShapeDtypeStruct((keep, per, n), jnp.float32),
            jax.ShapeDtypeStruct((per, TOPK), jnp.float32),
        ),
        in_specs=[vmem],
        out_specs=(vmem, vmem),
    )(inbox)


def local(
    queries,
    centroids,
    shard_table,
    token_refs,
    packed_residual_buckets,
    passage_lengths,
    bucket_values,
    candidates,
    live_counts,
):
    n, nz = lax.axis_size("cent"), lax.axis_size("qry")
    per, tokens, width = queries.shape[1:]
    wanted = shard_table.reshape(CENT_AXES[0], n // CENT_AXES[0], nz, -1)
    cand, live = candidates[0, 0].T, live_counts[0]
    table, resid, rows, order, members, place = fetch(
        centroids, wanted, queries.reshape(per * tokens, width), passage_lengths[None, :], packed_residual_buckets,
        bucket_values, cand, live,
    )
    tops = score(
        table.reshape(-1, width), token_refs, order, members, place, resid, rows.reshape(-1, width), cand, live
    )
    shard_tops, best_scores = merge(swap(tops, per), candidates.shape[3] // 4)
    return (jnp.transpose(shard_tops, (1, 2, 0))[None], best_scores[None])


def solution(mesh):
    return jax.shard_map(
        local,
        mesh=mesh,
        in_specs=(
            P("qry", "cent", None, None),
            P("cent", None),
            P("cent", None),
            P("cent", None),
            P("cent", None, None),
            P("cent"),
            P(),
            P("qry", "cent", None, None),
            P("qry", "cent", None),
        ),
        out_specs=(P("qry", "cent", None, None), P("qry", "cent", None)),
        check_vma=False,
    )
```
